256 devices in a mesh: beam: 2 (over x_lo), row: 2 (over core), col: 64 (over z, y, x_hi).
Axes of the slice: x: 4 (x_hi: 2, x_lo: 2; x = x_hi * 2 + x_lo), y: 4, z: 8, core: 2. Of those that a mesh axis runs over, the one named last changes fastest.
Arguments:
- transmission: float32 [2, 2, 512, 16384], P(None, 'beam', 'row', 'col')
- probe_field: float32 [2, 256, 256], replicated, may hold values from -4.2 to 4.2
- propagator: float32 [2, 256, 256], replicated
- intensities: float32 [256, 256, 256], P(('row', 'col')), may hold values from 0 to 3
- positions: int32 [256, 2], P(('row', 'col')), may hold values from 128 to 16256, as said below
- live_slots: int32 [256], P(('row', 'col')), may hold values from 0 to 1, as said below
Outputs:
- gradient: float32 [2, 2, 512, 16384], P(None, 'beam', 'row', 'col')
The draws below stay inside these ranges and needn't reach their ends.
Inputs may be any that keep to these rules, and one draw needn't show every extreme that they name: `positions`: each probe's center lies in the lateral tile of 256 x 256 cells of the device that holds its slot, and its footprint of 256 x 256 cells lies inside the object. `live_slots`: 1 marks a probe of the batch, 0 an empty slot; on each device the live slots come first, each device has one or more, and some device has all 2 live.
All inputs are finite; a program needn't handle non-finite values.
Results may differ from the reference program's by a relative error of at most 0.0003.
Values sent between devices are 32-bit elements; how exact they have to be, the bound alone decides.
A program may use at most 64 MiB of HBM per device.

```python
import jax
import jax.numpy as jnp
from jax import lax

PROBE_SIDE = 256
HALF_SIDE = 128
TILE_SIDE = 256
SLOT_DEV = 2
SLICES = 2
PROBES = 256
GRID_ROWS = 512
GRID_COLS = 16384
N_ROW = 2
N_COL = 64


def draw_transmission(key, part):
    key = jax.random.fold_in(key, 11)
    first_key, second_key = jax.random.split(key)
    shape = (SLICES, GRID_ROWS, GRID_COLS)
    real_part = jax.random.uniform(first_key, shape, jnp.float32, 0.8, 1.1)
    imag_part = 0.3 * jax.random.truncated_normal(second_key, -3.0, 3.0, shape, jnp.float32)
    return jnp.stack([real_part, imag_part]).astype(jnp.float32)


def draw_propagator(key, part):
    key = jax.random.fold_in(key, 23)
    shape = (2, PROBE_SIDE, PROBE_SIDE)
    rough = jax.random.truncated_normal(key, -4.0, 4.0, shape, jnp.float32)
    rough = rough * (0.35 / jnp.sqrt(jnp.float32(PROBE_SIDE)))
    identity = jnp.eye(PROBE_SIDE, dtype=jnp.float32)
    matrix = jnp.stack([identity + rough[0], rough[1]])
    return (matrix / jnp.sqrt(jnp.float32(1.245))).astype(jnp.float32)


def draw_positions(key, part):
    key = jax.random.fold_in(key, 37)
    first_key, second_key = jax.random.split(key)
    counter = jnp.arange(PROBES, dtype=jnp.int32)
    tile_at = counter // SLOT_DEV
    slot_at = counter % SLOT_DEV
    tiles = N_ROW * N_COL
    pin_low = (tile_at == 0) & (slot_at == 0)
    pin_high = (tile_at == tiles - 1) & (slot_at == 0)

    def coordinate(sub_key, block, count):
        lower = jnp.where(block == 0, HALF_SIDE, 0)
        upper = jnp.where(block == count - 1, TILE_SIDE - HALF_SIDE, TILE_SIDE - 1)
        picked = jax.random.randint(sub_key, (PROBES,), 0, TILE_SIDE * 64, dtype=jnp.int32)
        value = lower + picked % (upper - lower + 1)
        value = jnp.where(pin_low, lower, jnp.where(pin_high, upper, value))
        return block * TILE_SIDE + value
    row_value = coordinate(first_key, tile_at // N_COL, N_ROW)
    col_value = coordinate(second_key, tile_at % N_COL, N_COL)
    return jnp.stack([row_value, col_value], axis=1).astype(jnp.int32)


def draw_live_slots(key, part):
    key = jax.random.fold_in(key, 41)
    first_key, second_key = jax.random.split(key)
    tiles = N_ROW * N_COL
    counts = jax.random.randint(first_key, (tiles,), 1, SLOT_DEV + 1, dtype=jnp.int32)
    chosen = jax.random.randint(second_key, (), 0, tiles, dtype=jnp.int32)
    counts = jnp.where(jnp.arange(tiles, dtype=jnp.int32) == chosen, SLOT_DEV, counts)
    counter = jnp.arange(PROBES, dtype=jnp.int32)
    return (counter % SLOT_DEV < counts[counter // SLOT_DEV]).astype(jnp.int32)


def block_scale(rng, extent, cuts, smallest, top_value):
    def one(axis_at, parts):
        heights = jax.random.uniform(jax.random.fold_in(jax.random.fold_in(rng, 6), axis_at), (parts,), jnp.float32, smallest / len(cuts), top_value / len(cuts))
        return jnp.repeat(jnp.exp(heights), extent[axis_at] // parts).reshape((-1,) + (1,) * (len(extent) - axis_at - 1))

    loudness = one(*cuts[0])
    for cut in cuts[1:]:
        loudness = loudness * one(*cut)
    return loudness


def normal_values(own_key, extent, spread, limit, kind=jnp.bfloat16):
    result = spread * jax.random.normal(own_key, extent, jnp.float32)
    return jnp.clip(result, min=-limit, max=limit).astype(kind)


def setup_inputs(seed: int = 0) -> dict:
    key_list = jax.random.split(jax.random.key(seed), 7)
    transmission = draw_transmission(jax.random.fold_in(key_list[6], 71), 0)
    probe_field = normal_values(key_list[1], (2, PROBE_SIDE, PROBE_SIDE), 0.7, 4.2, jnp.float32)
    propagator = draw_propagator(jax.random.fold_in(key_list[6], 71), 0)
    intensities = jnp.clip(3.0 * jax.random.uniform(key_list[3], (PROBES, PROBE_SIDE, PROBE_SIDE), jnp.float32) ** block_scale(key_list[3], (PROBES, PROBE_SIDE, PROBE_SIDE), ((0, 128),), -0.2, 0.2), 0.0, 3.0)
    positions = draw_positions(jax.random.fold_in(key_list[6], 71), 0)
    live_slots = draw_live_slots(jax.random.fold_in(key_list[6], 71), 0)
    return dict(transmission=transmission, probe_field=probe_field, propagator=propagator, intensities=intensities, positions=positions, live_slots=live_slots)


HIGHEST = lax.Precision.HIGHEST

def plain_product(left_side, right_side):
    return jnp.dot(left_side, right_side, precision=HIGHEST, preferred_element_type=jnp.float32)

def complex_matmul(first, second):
    real_part = plain_product(first[0], second[0]) - plain_product(first[1], second[1])
    imag_part = plain_product(first[0], second[1]) + plain_product(first[1], second[0])
    return jnp.stack([real_part, imag_part])

def conjugate(matrix):
    return jnp.stack([matrix[0], -matrix[1]])

def transposed(matrix):
    return jnp.swapaxes(matrix, 1, 2)

def elementwise_times(first, second):
    return jnp.stack([first[0] * second[0] - first[1] * second[1], first[0] * second[1] + first[1] * second[0]])

def conj_times(first, second):
    return jnp.stack([first[0] * second[0] + first[1] * second[1], first[0] * second[1] - first[1] * second[0]])

def transform_table(side):
    counter = jnp.arange(side, dtype=jnp.int32)
    product = counter[:, None] * counter[None, :] % side
    angles = 2.0 * jnp.pi / side * product.astype(jnp.float32)
    scaling = 1.0 / jnp.sqrt(jnp.float32(side))
    return jnp.stack([jnp.cos(angles) * scaling, -jnp.sin(angles) * scaling])

def reference(transmission, probe_field, propagator, intensities, positions, live_slots):
    side = probe_field.shape[1]
    half = side // 2
    slices_all = transmission.shape[1]
    table = transform_table(side)
    table_conj = conjugate(table)
    kernel_t = transposed(propagator)
    kernel_h = conjugate(kernel_t)
    kernel_c = conjugate(propagator)

    def one_probe(total, item):
        centre, live_one, measured = item
        start = (jnp.int32(0), jnp.int32(0), (centre[0] - half).astype(jnp.int32), (centre[1] - half).astype(jnp.int32))
        window = lax.dynamic_slice(transmission, start, (2, slices_all, side, side))

        def forward_layer(slice_at, carry):
            wave, stored = carry
            stored = lax.dynamic_update_index_in_dim(stored, wave, slice_at, 0)
            trans = lax.dynamic_index_in_dim(window, slice_at, 1, keepdims=False)
            mixed = elementwise_times(trans, wave)
            wave = complex_matmul(complex_matmul(propagator, mixed), kernel_t)
            return (wave, stored)
        stored = jnp.zeros((slices_all, 2, side, side), jnp.float32)
        exit_wave, stored = lax.fori_loop(0, slices_all, forward_layer, (probe_field, stored))
        far = complex_matmul(complex_matmul(table, exit_wave), table)
        residual = live_one.astype(jnp.float32) * (far[0] * far[0] + far[1] * far[1] - measured)
        chi = complex_matmul(complex_matmul(table_conj, residual[None] * far), table_conj)

        def backward_layer(counter, carry):
            chi_now, pieces = carry
            slice_at = slices_all - 1 - counter
            back = complex_matmul(complex_matmul(kernel_h, chi_now), kernel_c)
            wave = lax.dynamic_index_in_dim(stored, slice_at, 0, keepdims=False)
            trans = lax.dynamic_index_in_dim(window, slice_at, 1, keepdims=False)
            piece = conj_times(wave, back)
            pieces = lax.dynamic_update_index_in_dim(pieces, piece, slice_at, 1)
            return (conj_times(trans, back), pieces)
        pieces = jnp.zeros((2, slices_all, side, side), jnp.float32)
        chi, pieces = lax.fori_loop(0, slices_all, backward_layer, (chi, pieces))
        current = lax.dynamic_slice(total, start, (2, slices_all, side, side))
        total = lax.dynamic_update_slice(total, current + pieces, start)
        return (total, jnp.float32(0.0))
    total = jnp.zeros(transmission.shape, jnp.float32)
    total, unused = lax.scan(one_probe, total, (positions, live_slots, intensities))
    return total
```

```python
import functools

import jax
import jax.numpy as jnp
import numpy as np
from jax import lax
from jax.experimental import pallas as pl
from jax.experimental.pallas import tpu as pltpu
from jax.sharding import PartitionSpec as P

MESH = pl.DeviceIdType.MESH
SIDE = 256
HALF = 128
F32 = jnp.float32
BF16 = jnp.bfloat16

TILE = 0
LEFTWARD = 4
RIGHTWARD = 6
RELAY_RIGHT = 8
RELAY_BEAM = 10
ROW = 12
GRAD_ROW = 20
GRAD_COL = 24
COPIES = 28


def transform_table(side):
    counter = np.arange(side)
    angles = 2.0 * np.pi / side * (counter[:, None] * counter[None, :] % side)
    return np.stack([np.cos(angles), -np.sin(angles)]).astype(np.float32) / np.float32(np.sqrt(side))


def split(value):
    high = value.astype(BF16)
    return high, (value - high.astype(F32)).astype(BF16)


def put_operator(operators, at, real, imag):
    real_high, real_low = split(real)
    imag_high, imag_low = split(imag)
    top = (real_high, real_high, real_low, -imag_high, -imag_high, -imag_low)
    low = (imag_high, imag_high, imag_low, real_high, real_high, real_low)
    for block in range(6):
        columns = slice(block * SIDE, (block + 1) * SIDE)
        operators[at, :SIDE, columns] = top[block]
        operators[at, SIDE:, columns] = low[block]


def kernel(
    cols,
    pos,
    live,
    trans,
    probe_hbm,
    prop_hbm,
    table_hbm,
    intens_hbm,
    out,
    ext,
    probe,
    prop,
    table,
    intens,
    operators,
    parts,
    wave,
    psi,
    window,
    pad,
    grad,
    grad_rows,
    grad_cols,
    local_sem,
    send_sem,
    recv_sem,
):
    beam, row, col = lax.axis_index("beam"), lax.axis_index("row"), lax.axis_index("col")
    other = 1 - beam
    has_left, has_right = col > 0, col < cols - 1
    partner = (other, row, col)
    sibling = (beam, 1 - row, col)
    left = (other, row, jnp.maximum(col - 1, 0))
    right = (other, row, jnp.minimum(col + 1, cols - 1))

    barrier = pltpu.get_barrier_semaphore()

    def greet(peer):
        pl.semaphore_signal(barrier, inc=1, device_id=peer, device_id_type=MESH)

    greet(partner)
    greet(sibling)
    pl.when(has_left)(lambda: greet(left))
    pl.when(has_right)(lambda: greet(right))

    def rows(start):
        return pl.ds(pl.multiple_of(start, HALF), HALF)

    tile_rows = (rows(HALF * (1 - row)), rows(HALF * row))
    ext_rows = (rows(jnp.int32(HALF)), rows(2 * HALF * row))
    sibling_rows = rows(2 * HALF * row)

    locals_ = [
        pltpu.make_async_copy(
            trans.at[:, 0, :, pl.ds(HALF * k, HALF)],
            ext.at[beam, 1 + k, :, pl.ds(pl.multiple_of(HALF * row, HALF), SIDE), :],
            local_sem.at[k],
        )
        for k in range(2)
    ]
    for at, (source, target) in enumerate(
        ((prop_hbm, prop), (table_hbm, table), (probe_hbm, probe), (intens_hbm, intens))
    ):
        locals_.append(pltpu.make_async_copy(source, target, local_sem.at[2 + at]))
    for copy in locals_:
        copy.start()

    def remote(at, source, target, peer):
        return pltpu.make_async_remote_copy(
            src_ref=source,
            dst_ref=target,
            send_sem=send_sem.at[at],
            recv_sem=recv_sem.at[at],
            device_id=peer,
            device_id_type=MESH,
        )

    def own(k, h):
        return trans.at[:, 0, tile_rows[h], pl.ds(HALF * k, HALF)]

    def block(of, k, h):
        return ext.at[of, k, :, ext_rows[h], :]

    tile = [[remote(TILE + 2 * k + h, own(k, h), block(beam, 1 + k, h), partner) for h in range(2)] for k in range(2)]
    leftward = [remote(LEFTWARD + h, own(0, h), block(beam, 3, h), left) for h in range(2)]
    rightward = [remote(RIGHTWARD + h, own(1, h), block(beam, 0, h), right) for h in range(2)]
    relay_right = [remote(RELAY_RIGHT + h, block(other, 2, h), block(other, 0, h), right) for h in range(2)]
    relay_beam = [remote(RELAY_BEAM + h, block(other, 3, h), block(other, 3, h), partner) for h in range(2)]

    def to_sibling(at, of, k, source=None):
        return remote(
            ROW + at, block(of, k, 0) if source is None else source, ext.at[of, k, :, sibling_rows, :], sibling
        )

    row_own = [to_sibling(k, beam, 1 + k, own(k, 0)) for k in range(2)]
    row_other = [to_sibling(2 + k, other, 1 + k) for k in range(2)]
    row_left_other = to_sibling(4, other, 0)
    row_left_own = to_sibling(5, beam, 0)
    row_right_other = to_sibling(6, other, 3)
    row_right_own = to_sibling(7, beam, 3)

    pl.semaphore_wait(barrier, 2 + jnp.where(has_left, 1, 0) + jnp.where(has_right, 1, 0))

    for h in range(2):
        tile[1][h].start()
        pl.when(has_left)(leftward[h].start)
    for h in range(2):
        tile[0][h].start()
        pl.when(has_right)(rightward[h].start)
    for k in range(2):
        row_own[k].start()

    for copy in locals_:
        copy.wait()
    put_operator(operators, 0, prop[0], prop[1])
    put_operator(operators, 1, prop[0].T, -prop[1].T)

    def then(copy, *followers):
        copy.wait_recv()
        for follower in followers:
            follower.start()

    def tile_right(h):
        tile[1][h].wait_recv()
        pl.when(has_right)(relay_right[h].start)
        if h == 0:
            row_other[1].start()

    def from_right(h):
        then(leftward[h], relay_beam[h], *((row_right_other,) if h == 0 else ()))

    for h in range(2):
        tile_right(h)
        pl.when(has_right)(functools.partial(from_right, h))

    put_operator(operators, 2, table[0], table[1])
    put_operator(operators, 3, table[0], -table[1])
    edge = jnp.zeros((2, 4 * HALF, HALF), F32)
    strip = jnp.zeros((2, HALF, HALF), F32)
    for slot in range(2):
        pad[slot, 0] = edge
        pad[slot, 4] = edge
        for k in range(1, 4):
            pad[slot, k, :, :HALF] = strip
            pad[slot, k, :, 3 * HALF :] = strip

    side_zero = jnp.zeros((2, 2, 3 * HALF, HALF), F32)

    @pl.when(jnp.logical_not(has_left))
    def _():
        ext[:, 0] = side_zero

    @pl.when(jnp.logical_not(has_right))
    def _():
        ext[:, 3] = side_zero

    then(tile[0][0], row_other[0])

    @pl.when(has_left)
    def _():
        then(rightward[0], row_left_other)

    then(tile[0][1])

    @pl.when(has_left)
    def _():
        then(rightward[1])
        then(relay_right[0], row_left_own)

    @pl.when(has_right)
    def _():
        then(relay_beam[0], row_right_own)

    @pl.when(has_left)
    def _():
        relay_right[1].wait_recv()

    @pl.when(has_right)
    def _():
        relay_beam[1].wait_recv()

    for k in range(2):
        row_own[k].wait_recv()
        row_other[k].wait_recv()

    @pl.when(has_left)
    def _():
        row_left_other.wait_recv()
        row_left_own.wait_recv()

    @pl.when(has_right)
    def _():
        row_right_other.wait_recv()
        row_right_own.wait_recv()

    row_at = [jnp.clip(pos[slot, 0] - HALF - HALF * row, 0, HALF) for slot in range(2)]
    col_at = [jnp.clip(pos[slot, 1] - SIDE * col, 0, SIDE - 1) for slot in range(2)]
    block_at = [at // HALF for at in col_at]
    lane_at = [at % HALF for at in col_at]
    lanes = lax.broadcasted_iota(jnp.int32, (SIDE, HALF), 1)

    def footprint(of, slot, part):
        back = lax.rem(HALF - lane_at[slot], HALF)
        turned = [
            pltpu.roll(ext[of, block_at[slot] + j, part, pl.ds(row_at[slot], SIDE), :], back, 1) for j in range(3)
        ]
        near = lanes < HALF - lane_at[slot]
        return [jnp.where(near, turned[j], turned[j + 1]) for j in range(2)]

    def spread(operator):
        def stage(counter, carry):
            for slot in range(2):
                for part in range(2):
                    high, low = split(wave[slot, SIDE * part : SIDE * (part + 1)])
                    start = 3 * SIDE * part
                    parts[slot, :, start : start + SIDE] = high
                    parts[slot, :, start + SIDE : start + 2 * SIDE] = low
                    parts[slot, :, start + 2 * SIDE : start + 3 * SIDE] = high
                wave[slot] = lax.dot_general(
                    operators[operator], parts[slot], (((1,), (1,)), ((), ())), preferred_element_type=F32
                )
            return carry

        lax.fori_loop(0, 2, stage, 0)

    real, imag = slice(0, SIDE), slice(SIDE, 2 * SIDE)

    for slot in range(2):
        window_real, window_imag = footprint(0, slot, 0), footprint(0, slot, 1)
        for j in range(2):
            at = slice(j * HALF, (j + 1) * HALF)
            probe_real, probe_imag = probe[0, :, at], probe[1, :, at]
            wave[slot, real, at] = window_real[j] * probe_real - window_imag[j] * probe_imag
            wave[slot, imag, at] = window_real[j] * probe_imag + window_imag[j] * probe_real
    spread(0)
    for slot in range(2):
        window_real, window_imag = footprint(1, slot, 0), footprint(1, slot, 1)
        for j in range(2):
            at = slice(j * HALF, (j + 1) * HALF)
            wave_real, wave_imag = wave[slot, real, at], wave[slot, imag, at]
            psi[slot, real, at], psi[slot, imag, at] = wave_real, wave_imag
            window[slot, real, at], window[slot, imag, at] = window_real[j], window_imag[j]
            wave[slot, real, at] = window_real[j] * wave_real - window_imag[j] * wave_imag
            wave[slot, imag, at] = window_real[j] * wave_imag + window_imag[j] * wave_real
    spread(0)
    spread(2)
    for slot in range(2):
        far_real, far_imag = wave[slot, real], wave[slot, imag]
        weight = live[slot].astype(F32)
        residual = weight * (far_real * far_real + far_imag * far_imag - intens[slot])
        wave[slot, real] = residual * far_real
        wave[slot, imag] = residual * far_imag
    spread(3)
    spread(1)

    middle = slice(HALF, 3 * HALF)

    def place(slot, part, pieces):
        turned = [pltpu.roll(piece, lane_at[slot], 1) for piece in pieces]
        inside = lanes >= lane_at[slot]
        zero = jnp.zeros_like(turned[0])
        pad[slot, 1, part, middle] = jnp.where(inside, turned[0], zero)
        pad[slot, 2, part, middle] = jnp.where(inside, turned[1], turned[0])
        pad[slot, 3, part, middle] = jnp.where(inside, zero, turned[1])

    def collect(of):
        core = jnp.where(beam == of, 1, 0)
        for side in range(2):
            at = jnp.where(beam == of, 1 + side, 3 * side)
            for part in range(2):
                terms = [
                    pad[slot, at + 1 - block_at[slot], part, pl.ds(HALF - row_at[slot], 3 * HALF), :]
                    for slot in range(2)
                ]
                grad[core, side, part] = terms[0] + terms[1]

    def gradient(slot, lit_real, lit_imag):
        pieces = ([], [])
        for j in range(2):
            at = slice(j * HALF, (j + 1) * HALF)
            back_real, back_imag = wave[slot, real, at], wave[slot, imag, at]
            first, second = lit_real(at), lit_imag(at)
            pieces[0].append(first * back_real + second * back_imag)
            pieces[1].append(first * back_imag - second * back_real)
        place(slot, 0, pieces[0])
        place(slot, 1, pieces[1])

    away_rows = rows(2 * HALF * (1 - row))
    grad_row = [
        [
            remote(GRAD_ROW + 2 * core + side, grad.at[core, side, :, away_rows, :], grad_rows.at[core, side], sibling)
            for side in range(2)
        ]
        for core in range(2)
    ]
    grad_col = [
        [
            remote(
                GRAD_COL + 2 * side + h,
                grad.at[0, side, :, ext_rows[h], :],
                grad_cols.at[side, h],
                right if side else left,
            )
            for h in range(2)
        ]
        for side in range(2)
    ]
    has_side = (has_left, has_right)

    def send_halo():
        for side in range(2):
            grad_row[0][side].start()
            pl.when(has_side[side])(grad_col[side][1].start)

    for slot in range(2):
        gradient(slot, lambda at: psi[slot, real, at], lambda at: psi[slot, imag, at])
        back_real, back_imag = wave[slot, real], wave[slot, imag]
        window_real, window_imag = window[slot, real], window[slot, imag]
        wave[slot, real] = window_real * back_real + window_imag * back_imag
        wave[slot, imag] = window_real * back_imag - window_imag * back_real
    collect(1)
    pl.when(beam == 0)(send_halo)
    spread(1)
    for slot in range(2):
        gradient(slot, lambda at: probe[0, :, at], lambda at: probe[1, :, at])
    collect(0)
    pl.when(beam == 1)(send_halo)
    for side in range(2):
        grad_row[1][side].start()
    for side in range(2):
        grad_row[0][side].wait_recv()

        @pl.when(has_side[side])
        def _():
            grad[0, side, :, HALF : 2 * HALF] += grad_rows[0, side]
            grad_col[side][0].start()

    for side in range(2):
        at = slice(side * HALF, (side + 1) * HALF)
        grad_row[1][side].wait_recv()
        out[:, 0, tile_rows[0], at] = grad[1, side, :, HALF : 2 * HALF] + grad_rows[1, side]
        out[:, 0, tile_rows[1], at] = grad[1, side, :, ext_rows[1]]
    for h in (1, 0):
        for side in range(2):
            at = slice(side * HALF, (side + 1) * HALF)

            @pl.when(has_side[side])
            def _():
                grad_col[1 - side][h].wait_recv()
                out[:, 0, tile_rows[h], at] += grad_cols[1 - side, h]

    for h in range(2):
        for k in range(2):
            tile[k][h].wait_send()
    for k in range(2):
        row_own[k].wait_send()
        row_other[k].wait_send()
        for core in range(2):
            grad_row[core][k].wait_send()

    @pl.when(has_left)
    def _():
        row_left_other.wait_send()
        row_left_own.wait_send()
        for h in range(2):
            leftward[h].wait_send()
            grad_col[0][h].wait_send()

    @pl.when(has_right)
    def _():
        row_right_other.wait_send()
        row_right_own.wait_send()
        for h in range(2):
            rightward[h].wait_send()
            relay_right[h].wait_send()
            relay_beam[h].wait_send()
            grad_col[1][h].wait_send()


def body(cols, transmission, probe_field, propagator, intensities, positions, live_slots):
    anywhere = pl.BlockSpec(memory_space=pl.ANY)
    scalars = pl.BlockSpec(memory_space=pltpu.SMEM)
    plane = (2, SIDE, SIDE)
    stacked = (2, 2 * SIDE, SIDE)
    return pl.pallas_call(
        functools.partial(kernel, cols),
        out_shape=jax.ShapeDtypeStruct((2, 1, SIDE, SIDE), F32),
        in_specs=[scalars, scalars] + [anywhere] * 5,
        out_specs=pl.BlockSpec(memory_space=pltpu.VMEM),
        scratch_shapes=[
            pltpu.VMEM((2, 4, 2, 3 * HALF, HALF), F32),
            pltpu.VMEM(plane, F32),
            pltpu.VMEM(plane, F32),
            pltpu.VMEM(plane, F32),
            pltpu.VMEM(plane, F32),
            pltpu.VMEM((4, 2 * SIDE, 6 * SIDE), BF16),
            pltpu.VMEM((2, SIDE, 6 * SIDE), BF16),
            pltpu.VMEM(stacked, F32),
            pltpu.VMEM(stacked, F32),
            pltpu.VMEM(stacked, F32),
            pltpu.VMEM((2, 5, 2, 4 * HALF, HALF), F32),
            pltpu.VMEM((2, 2, 2, 3 * HALF, HALF), F32),
            pltpu.VMEM((2, 2, 2, HALF, HALF), F32),
            pltpu.VMEM((2, 2, 2, HALF, HALF), F32),
            pltpu.SemaphoreType.DMA((6,)),
            pltpu.SemaphoreType.DMA((COPIES,)),
            pltpu.SemaphoreType.DMA((COPIES,)),
        ],
        compiler_params=pltpu.CompilerParams(
            collective_id=0, has_side_effects=True, vmem_limit_bytes=48 * 1024 * 1024
        ),
    )(
        positions,
        live_slots,
        transmission,
        probe_field,
        propagator,
        jnp.asarray(transform_table(SIDE)),
        intensities,
    )


def solution(mesh):
    return jax.shard_map(
        functools.partial(body, mesh.shape["col"]),
        mesh=mesh,
        in_specs=(
            P(None, "beam", "row", "col"),
            P(),
            P(),
            P(("row", "col"), None, None),
            P(("row", "col"), None),
            P(("row", "col")),
        ),
        out_specs=P(None, "beam", "row", "col"),
        check_vma=False,
    )
```

```python
import functools

import jax
import jax.numpy as jnp
import numpy as np
from jax import lax
from jax.experimental import pallas as pl
from jax.experimental.pallas import tpu as pltpu
from jax.sharding import PartitionSpec as P

MESH = pl.DeviceIdType.MESH
SIDE = 256
HALF = 128
F32 = jnp.float32
BF16 = jnp.bfloat16

TILE = 0
LEFTWARD = 4
RIGHTWARD = 6
RELAY_RIGHT = 8
RELAY_BEAM = 10
ROW = 12
GRAD_ROW = 20
GRAD_COL = 24
COPIES = 28


def transform_table(side):
    counter = np.arange(side)
    angles = 2.0 * np.pi / side * (counter[:, None] * counter[None, :] % side)
    return np.stack([np.cos(angles), -np.sin(angles)]).astype(np.float32) / np.float32(np.sqrt(side))


def split(value):
    high = value.astype(BF16)
    return high, (value - high.astype(F32)).astype(BF16)


def put_operator(operators, at, real, imag):
    real_high, real_low = split(real)
    imag_high, imag_low = split(imag)
    top = (real_high, real_high, real_low, -imag_high, -imag_high, -imag_low)
    low = (imag_high, imag_high, imag_low, real_high, real_high, real_low)
    for block in range(6):
        columns = slice(block * SIDE, (block + 1) * SIDE)
        operators[at, :SIDE, columns] = top[block]
        operators[at, SIDE:, columns] = low[block]


def kernel(
    cols,
    pos_hbm,
    live_hbm,
    trans,
    probe_hbm,
    prop_hbm,
    table_hbm,
    intens_hbm,
    out,
    pos,
    live,
    ext,
    probe,
    prop,
    table,
    intens,
    operators,
    parts,
    wave,
    psi,
    window,
    pad,
    grad,
    grad_rows,
    grad_cols,
    local_sem,
    send_sem,
    recv_sem,
):
    beam, row, col = lax.axis_index("beam"), lax.axis_index("row"), lax.axis_index("col")
    other = 1 - beam
    has_left, has_right = col > 0, col < cols - 1
    partner = (other, row, col)
    sibling = (beam, 1 - row, col)
    left = (other, row, jnp.maximum(col - 1, 0))
    right = (other, row, jnp.minimum(col + 1, cols - 1))

    barrier = pltpu.get_barrier_semaphore()

    def greet(peer):
        pl.semaphore_signal(barrier, inc=1, device_id=peer, device_id_type=MESH)

    greet(partner)
    greet(sibling)
    pl.when(has_left)(lambda: greet(left))
    pl.when(has_right)(lambda: greet(right))

    def rows(start):
        return pl.ds(pl.multiple_of(start, HALF), HALF)

    tile_rows = (rows(HALF * (1 - row)), rows(HALF * row))
    ext_rows = (rows(jnp.int32(HALF)), rows(2 * HALF * row))
    sibling_rows = rows(2 * HALF * row)

    locals_ = [
        pltpu.make_async_copy(
            trans.at[:, 0, :, pl.ds(HALF * k, HALF)],
            ext.at[beam, 1 + k, :, pl.ds(pl.multiple_of(HALF * row, HALF), SIDE), :],
            local_sem.at[k],
        )
        for k in range(2)
    ]
    for at, (source, target) in enumerate(
        ((prop_hbm, prop), (table_hbm, table), (probe_hbm, probe), (intens_hbm, intens), (pos_hbm, pos), (live_hbm, live))
    ):
        locals_.append(pltpu.make_async_copy(source, target, local_sem.at[2 + at]))
    for copy in locals_:
        copy.start()

    def remote(at, source, target, peer):
        return pltpu.make_async_remote_copy(
            src_ref=source,
            dst_ref=target,
            send_sem=send_sem.at[at],
            recv_sem=recv_sem.at[at],
            device_id=peer,
            device_id_type=MESH,
        )

    def own(k, h):
        return trans.at[:, 0, tile_rows[h], pl.ds(HALF * k, HALF)]

    def block(of, k, h):
        return ext.at[of, k, :, ext_rows[h], :]

    tile = [[remote(TILE + 2 * k + h, own(k, h), block(beam, 1 + k, h), partner) for h in range(2)] for k in range(2)]
    leftward = [remote(LEFTWARD + h, own(0, h), block(beam, 3, h), left) for h in range(2)]
    rightward = [remote(RIGHTWARD + h, own(1, h), block(beam, 0, h), right) for h in range(2)]
    relay_right = [remote(RELAY_RIGHT + h, block(other, 2, h), block(other, 0, h), right) for h in range(2)]
    relay_beam = [remote(RELAY_BEAM + h, block(other, 3, h), block(other, 3, h), partner) for h in range(2)]

    def to_sibling(at, of, k, source=None):
        return remote(
            ROW + at, block(of, k, 0) if source is None else source, ext.at[of, k, :, sibling_rows, :], sibling
        )

    row_own = [to_sibling(k, beam, 1 + k, own(k, 0)) for k in range(2)]
    row_other = [to_sibling(2 + k, other, 1 + k) for k in range(2)]
    row_left_other = to_sibling(4, other, 0)
    row_left_own = to_sibling(5, beam, 0)
    row_right_other = to_sibling(6, other, 3)
    row_right_own = to_sibling(7, beam, 3)

    pl.semaphore_wait(barrier, 2 + jnp.where(has_left, 1, 0) + jnp.where(has_right, 1, 0))

    for h in range(2):
        tile[1][h].start()
        pl.when(has_left)(leftward[h].start)
    for h in range(2):
        tile[0][h].start()
        pl.when(has_right)(rightward[h].start)
    for k in range(2):
        row_own[k].start()

    for copy in locals_:
        copy.wait()
    put_operator(operators, 0, prop[0], prop[1])
    put_operator(operators, 1, prop[0].T, -prop[1].T)

    def then(copy, *followers):
        copy.wait_recv()
        for follower in followers:
            follower.start()

    def tile_right(h):
        tile[1][h].wait_recv()
        pl.when(has_right)(relay_right[h].start)
        if h == 0:
            row_other[1].start()

    def from_right(h):
        then(leftward[h], relay_beam[h], *((row_right_other,) if h == 0 else ()))

    for h in range(2):
        tile_right(h)
        pl.when(has_right)(functools.partial(from_right, h))

    put_operator(operators, 2, table[0], table[1])
    put_operator(operators, 3, table[0], -table[1])
    edge = jnp.zeros((2, 4 * HALF, HALF), F32)
    strip = jnp.zeros((2, HALF, HALF), F32)
    for slot in range(2):
        pad[slot, 0] = edge
        pad[slot, 4] = edge
        for k in range(1, 4):
            pad[slot, k, :, :HALF] = strip
            pad[slot, k, :, 3 * HALF :] = strip

    side_zero = jnp.zeros((2, 2, 3 * HALF, HALF), F32)

    @pl.when(jnp.logical_not(has_left))
    def _():
        ext[:, 0] = side_zero

    @pl.when(jnp.logical_not(has_right))
    def _():
        ext[:, 3] = side_zero

    then(tile[0][0], row_other[0])

    @pl.when(has_left)
    def _():
        then(rightward[0], row_left_other)

    then(tile[0][1])

    @pl.when(has_left)
    def _():
        then(rightward[1])
        then(relay_right[0], row_left_own)

    @pl.when(has_right)
    def _():
        then(relay_beam[0], row_right_own)

    @pl.when(has_left)
    def _():
        relay_right[1].wait_recv()

    @pl.when(has_right)
    def _():
        relay_beam[1].wait_recv()

    for k in range(2):
        row_own[k].wait_recv()
        row_other[k].wait_recv()

    @pl.when(has_left)
    def _():
        row_left_other.wait_recv()
        row_left_own.wait_recv()

    @pl.when(has_right)
    def _():
        row_right_other.wait_recv()
        row_right_own.wait_recv()

    row_at = [jnp.clip(pos[slot, 0] - HALF - HALF * row, 0, HALF) for slot in range(2)]
    col_at = [jnp.clip(pos[slot, 1] - SIDE * col, 0, SIDE - 1) for slot in range(2)]
    block_at = [at // HALF for at in col_at]
    lane_at = [at % HALF for at in col_at]
    lanes = lax.broadcasted_iota(jnp.int32, (SIDE, HALF), 1)

    def footprint(of, slot, part):
        back = lax.rem(HALF - lane_at[slot], HALF)
        turned = [
            pltpu.roll(ext[of, block_at[slot] + j, part, pl.ds(row_at[slot], SIDE), :], back, 1) for j in range(3)
        ]
        near = lanes < HALF - lane_at[slot]
        return [jnp.where(near, turned[j], turned[j + 1]) for j in range(2)]

    def spread(operator):
        def stage(counter, carry):
            for slot in range(2):
                for part in range(2):
                    high, low = split(wave[slot, SIDE * part : SIDE * (part + 1)])
                    start = 3 * SIDE * part
                    parts[slot, :, start : start + SIDE] = high
                    parts[slot, :, start + SIDE : start + 2 * SIDE] = low
                    parts[slot, :, start + 2 * SIDE : start + 3 * SIDE] = high
                wave[slot] = lax.dot_general(
                    operators[operator], parts[slot], (((1,), (1,)), ((), ())), preferred_element_type=F32
                )
            return carry

        lax.fori_loop(0, 2, stage, 0)

    real, imag = slice(0, SIDE), slice(SIDE, 2 * SIDE)

    for slot in range(2):
        window_real, window_imag = footprint(0, slot, 0), footprint(0, slot, 1)
        for j in range(2):
            at = slice(j * HALF, (j + 1) * HALF)
            probe_real, probe_imag = probe[0, :, at], probe[1, :, at]
            wave[slot, real, at] = window_real[j] * probe_real - window_imag[j] * probe_imag
            wave[slot, imag, at] = window_real[j] * probe_imag + window_imag[j] * probe_real
    spread(0)
    for slot in range(2):
        window_real, window_imag = footprint(1, slot, 0), footprint(1, slot, 1)
        for j in range(2):
            at = slice(j * HALF, (j + 1) * HALF)
            wave_real, wave_imag = wave[slot, real, at], wave[slot, imag, at]
            psi[slot, real, at], psi[slot, imag, at] = wave_real, wave_imag
            window[slot, real, at], window[slot, imag, at] = window_real[j], window_imag[j]
            wave[slot, real, at] = window_real[j] * wave_real - window_imag[j] * wave_imag
            wave[slot, imag, at] = window_real[j] * wave_imag + window_imag[j] * wave_real
    spread(0)
    spread(2)
    for slot in range(2):
        far_real, far_imag = wave[slot, real], wave[slot, imag]
        weight = live[slot].astype(F32)
        residual = weight * (far_real * far_real + far_imag * far_imag - intens[slot])
        wave[slot, real] = residual * far_real
        wave[slot, imag] = residual * far_imag
    spread(3)
    spread(1)

    middle = slice(HALF, 3 * HALF)

    def place(slot, part, pieces):
        turned = [pltpu.roll(piece, lane_at[slot], 1) for piece in pieces]
        inside = lanes >= lane_at[slot]
        zero = jnp.zeros_like(turned[0])
        pad[slot, 1, part, middle] = jnp.where(inside, turned[0], zero)
        pad[slot, 2, part, middle] = jnp.where(inside, turned[1], turned[0])
        pad[slot, 3, part, middle] = jnp.where(inside, zero, turned[1])

    def collect(of):
        core = jnp.where(beam == of, 1, 0)
        for side in range(2):
            at = jnp.where(beam == of, 1 + side, 3 * side)
            for part in range(2):
                terms = [
                    pad[slot, at + 1 - block_at[slot], part, pl.ds(HALF - row_at[slot], 3 * HALF), :]
                    for slot in range(2)
                ]
                grad[core, side, part] = terms[0] + terms[1]

    def gradient(slot, lit_real, lit_imag):
        pieces = ([], [])
        for j in range(2):
            at = slice(j * HALF, (j + 1) * HALF)
            back_real, back_imag = wave[slot, real, at], wave[slot, imag, at]
            first, second = lit_real(at), lit_imag(at)
            pieces[0].append(first * back_real + second * back_imag)
            pieces[1].append(first * back_imag - second * back_real)
        place(slot, 0, pieces[0])
        place(slot, 1, pieces[1])

    away_rows = rows(2 * HALF * (1 - row))
    grad_row = [
        [
            remote(GRAD_ROW + 2 * core + side, grad.at[core, side, :, away_rows, :], grad_rows.at[core, side], sibling)
            for side in range(2)
        ]
        for core in range(2)
    ]
    grad_col = [
        [
            remote(
                GRAD_COL + 2 * side + h,
                grad.at[0, side, :, ext_rows[h], :],
                grad_cols.at[side, h],
                right if side else left,
            )
            for h in range(2)
        ]
        for side in range(2)
    ]
    has_side = (has_left, has_right)

    def send_halo():
        for side in range(2):
            grad_row[0][side].start()
            pl.when(has_side[side])(grad_col[side][1].start)

    for slot in range(2):
        gradient(slot, lambda at: psi[slot, real, at], lambda at: psi[slot, imag, at])
        back_real, back_imag = wave[slot, real], wave[slot, imag]
        window_real, window_imag = window[slot, real], window[slot, imag]
        wave[slot, real] = window_real * back_real + window_imag * back_imag
        wave[slot, imag] = window_real * back_imag - window_imag * back_real
    collect(1)
    pl.when(beam == 0)(send_halo)
    spread(1)
    for slot in range(2):
        gradient(slot, lambda at: probe[0, :, at], lambda at: probe[1, :, at])
    collect(0)
    pl.when(beam == 1)(send_halo)
    for side in range(2):
        grad_row[1][side].start()
    for side in range(2):
        grad_row[0][side].wait_recv()

        @pl.when(has_side[side])
        def _():
            grad[0, side, :, HALF : 2 * HALF] += grad_rows[0, side]
            grad_col[side][0].start()

    for side in range(2):
        at = slice(side * HALF, (side + 1) * HALF)
        grad_row[1][side].wait_recv()
        out[:, 0, tile_rows[0], at] = grad[1, side, :, HALF : 2 * HALF] + grad_rows[1, side]
        out[:, 0, tile_rows[1], at] = grad[1, side, :, ext_rows[1]]
    for h in (1, 0):
        for side in range(2):
            at = slice(side * HALF, (side + 1) * HALF)

            @pl.when(has_side[side])
            def _():
                grad_col[1 - side][h].wait_recv()
                out[:, 0, tile_rows[h], at] += grad_cols[1 - side, h]

    for h in range(2):
        for k in range(2):
            tile[k][h].wait_send()
    for k in range(2):
        row_own[k].wait_send()
        row_other[k].wait_send()
        for core in range(2):
            grad_row[core][k].wait_send()

    @pl.when(has_left)
    def _():
        row_left_other.wait_send()
        row_left_own.wait_send()
        for h in range(2):
            leftward[h].wait_send()
            grad_col[0][h].wait_send()

    @pl.when(has_right)
    def _():
        row_right_other.wait_send()
        row_right_own.wait_send()
        for h in range(2):
            rightward[h].wait_send()
            relay_right[h].wait_send()
            relay_beam[h].wait_send()
            grad_col[1][h].wait_send()


def body(cols, transmission, probe_field, propagator, intensities, positions, live_slots):
    in_hbm = pl.BlockSpec(memory_space=pltpu.HBM)
    plane = (2, SIDE, SIDE)
    stacked = (2, 2 * SIDE, SIDE)
    return pl.pallas_call(
        functools.partial(kernel, cols),
        out_shape=jax.ShapeDtypeStruct((2, 1, SIDE, SIDE), F32),
        in_specs=[in_hbm] * 7,
        out_specs=pl.BlockSpec(memory_space=pltpu.VMEM),
        scratch_shapes=[
            pltpu.SMEM((2, 2), jnp.int32),
            pltpu.SMEM((2,), jnp.int32),
            pltpu.VMEM((2, 4, 2, 3 * HALF, HALF), F32),
            pltpu.VMEM(plane, F32),
            pltpu.VMEM(plane, F32),
            pltpu.VMEM(plane, F32),
            pltpu.VMEM(plane, F32),
            pltpu.VMEM((4, 2 * SIDE, 6 * SIDE), BF16),
            pltpu.VMEM((2, SIDE, 6 * SIDE), BF16),
            pltpu.VMEM(stacked, F32),
            pltpu.VMEM(stacked, F32),
            pltpu.VMEM(stacked, F32),
            pltpu.VMEM((2, 5, 2, 4 * HALF, HALF), F32),
            pltpu.VMEM((2, 2, 2, 3 * HALF, HALF), F32),
            pltpu.VMEM((2, 2, 2, HALF, HALF), F32),
            pltpu.VMEM((2, 2, 2, HALF, HALF), F32),
            pltpu.SemaphoreType.DMA((8,)),
            pltpu.SemaphoreType.DMA((COPIES,)),
            pltpu.SemaphoreType.DMA((COPIES,)),
        ],
        compiler_params=pltpu.CompilerParams(
            collective_id=0, has_side_effects=True, vmem_limit_bytes=60 * 1024 * 1024
        ),
    )(
        positions,
        live_slots,
        transmission,
        probe_field,
        propagator,
        jnp.asarray(transform_table(SIDE)),
        intensities,
    )


def solution(mesh):
    return jax.shard_map(
        functools.partial(body, mesh.shape["col"]),
        mesh=mesh,
        in_specs=(
            P(None, "beam", "row", "col"),
            P(),
            P(),
            P(("row", "col"), None, None),
            P(("row", "col"), None),
            P(("row", "col")),
        ),
        out_specs=P(None, "beam", "row", "col"),
        check_vma=False,
    )
```

```python
import functools

import jax
import jax.numpy as jnp
import numpy as np
from jax import lax
from jax.experimental import pallas as pl
from jax.experimental.pallas import tpu as pltpu
from jax.sharding import PartitionSpec as P

MESH = pl.DeviceIdType.MESH
SIDE = 256
HALF = 128
F32 = jnp.float32
BF16 = jnp.bfloat16

TILE = 0
LEFTWARD = 4
RIGHTWARD = 6
RELAY_RIGHT = 8
RELAY_BEAM = 10
ROW = 12
GRAD_ROW = 20
GRAD_COL = 24
COPIES = 28


def transform_table(side):
    counter = np.arange(side)
    angles = 2.0 * np.pi / side * (counter[:, None] * counter[None, :] % side)
    return np.stack([np.cos(angles), -np.sin(angles)]).astype(np.float32) / np.float32(np.sqrt(side))


def split(value):
    high = value.astype(BF16)
    return high, (value - high.astype(F32)).astype(BF16)


def put_operator(operators, at, real, imag, scale):
    real, imag = real * scale, imag * scale
    for which, value in enumerate((real, imag, real + imag)):
        high, low = split(value)
        for block, part in enumerate((high, high, low)):
            operators[at, which, :, block * SIDE : (block + 1) * SIDE] = part


def kernel(
    cols,
    pos_hbm,
    live_hbm,
    trans,
    probe_hbm,
    prop_hbm,
    table_hbm,
    intens_hbm,
    core_out,
    halo_out,
    pos,
    live,
    ext,
    whole,
    probe,
    prop,
    table,
    intens,
    operators,
    parts,
    wave,
    psi,
    window,
    pad,
    grad,
    grad_rows,
    core,
    zeros,
    local_sem,
    send_sem,
    recv_sem,
):
    beam, row, col = lax.axis_index("beam"), lax.axis_index("row"), lax.axis_index("col")
    other = 1 - beam
    first_slice, second_slice = beam == 0, beam == 1
    has_left, has_right = col > 0, col < cols - 1
    partner = (other, row, col)
    sibling = (beam, 1 - row, col)
    left = (other, row, jnp.maximum(col - 1, 0))
    right = (other, row, jnp.minimum(col + 1, cols - 1))

    barrier = pltpu.get_barrier_semaphore()

    def greet(peer):
        pl.semaphore_signal(barrier, inc=1, device_id=peer, device_id_type=MESH)

    greet(partner)
    greet(sibling)
    pl.when(has_left)(lambda: greet(left))
    pl.when(has_right)(lambda: greet(right))

    def rows(start):
        return pl.ds(pl.multiple_of(start, HALF), HALF)

    tile_rows = (rows(HALF * (1 - row)), rows(HALF * row))
    ext_rows = (rows(jnp.int32(HALF)), rows(2 * HALF * row))
    sibling_rows = rows(2 * HALF * row)

    locals_ = [
        pltpu.make_async_copy(
            trans.at[:, 0, :, pl.ds(HALF * k, HALF)],
            ext.at[beam, 1 + k, :, pl.ds(pl.multiple_of(HALF * row, HALF), SIDE), :],
            local_sem.at[k],
        )
        for k in range(2)
    ]
    for at, (source, target) in enumerate(
        ((prop_hbm, prop), (table_hbm, table), (probe_hbm, probe), (intens_hbm, intens), (pos_hbm, pos), (live_hbm, live))
    ):
        locals_.append(pltpu.make_async_copy(source, target, local_sem.at[2 + at]))
    for copy in locals_:
        copy.start()

    def remote(at, source, target, peer):
        return pltpu.make_async_remote_copy(
            src_ref=source,
            dst_ref=target,
            send_sem=send_sem.at[at],
            recv_sem=recv_sem.at[at],
            device_id=peer,
            device_id_type=MESH,
        )

    def own(k, h):
        return trans.at[:, 0, tile_rows[h], pl.ds(HALF * k, HALF)]

    def block(of, k, h):
        return ext.at[of, k, :, ext_rows[h], :]

    tile = [[remote(TILE + 2 * k + h, own(k, h), block(beam, 1 + k, h), partner) for h in range(2)] for k in range(2)]
    leftward = [remote(LEFTWARD + h, own(0, h), block(beam, 3, h), left) for h in range(2)]
    rightward = [remote(RIGHTWARD + h, own(1, h), block(beam, 0, h), right) for h in range(2)]
    relay_right = [remote(RELAY_RIGHT + h, block(other, 2, h), block(other, 0, h), right) for h in range(2)]
    relay_beam = [remote(RELAY_BEAM + h, block(other, 3, h), block(other, 3, h), partner) for h in range(2)]

    def to_sibling(at, of, k, source=None):
        return remote(
            ROW + at, block(of, k, 0) if source is None else source, ext.at[of, k, :, sibling_rows, :], sibling
        )

    row_own = [to_sibling(k, beam, 1 + k, own(k, 0)) for k in range(2)]
    row_other = [to_sibling(2 + k, other, 1 + k) for k in range(2)]
    row_left_other = to_sibling(4, other, 0)
    row_left_own = to_sibling(5, beam, 0)
    row_right_other = to_sibling(6, other, 3)
    row_right_own = to_sibling(7, beam, 3)

    pl.semaphore_wait(barrier, 2 + jnp.where(has_left, 1, 0) + jnp.where(has_right, 1, 0))

    for h in range(2):
        tile[1][h].start()
        pl.when(has_left)(leftward[h].start)
    for k in range(2):
        row_own[k].start()

    def send_rest(h):
        tile[0][h].start()
        pl.when(has_right)(rightward[h].start)

    def send_relays(h):
        tile[1][h].wait_recv()
        pl.when(has_right)(relay_right[h].start)
        if h == 0:
            row_other[1].start()

        @pl.when(has_right)
        def _():
            leftward[h].wait_recv()
            relay_beam[h].start()
            if h == 0:
                row_right_other.start()

    def rest_sent(h):
        tile[0][h].wait_send()
        pl.when(has_right)(rightward[h].wait_send)

    def relays_sent(h):
        @pl.when(has_right)
        def _():
            relay_right[h].wait_send()
            relay_beam[h].wait_send()

    def second(h):
        tile[1][h].wait_send()
        pl.when(has_left)(leftward[h].wait_send)
        pl.when(first_slice)(functools.partial(send_rest, h))
        pl.when(second_slice)(functools.partial(send_relays, h))

    def third(h):
        @pl.when(first_slice)
        def _():
            rest_sent(h)
            send_relays(h)

        @pl.when(second_slice)
        def _():
            relays_sent(h)
            send_rest(h)

    def own_edges():
        @pl.when(has_left)
        def _():
            relay_right[0].wait_recv()
            row_left_own.start()

        @pl.when(has_right)
        def _():
            relay_beam[0].wait_recv()
            row_right_own.start()

    def own_rest():
        for k in range(2):
            row_own[k].wait_recv()

        @pl.when(has_left)
        def _():
            relay_right[1].wait_recv()
            row_left_own.wait_recv()

        @pl.when(has_right)
        def _():
            relay_beam[1].wait_recv()
            row_right_own.wait_recv()

    def other_edges():
        tile[0][0].wait_recv()
        row_other[0].start()

        @pl.when(has_left)
        def _():
            rightward[0].wait_recv()
            row_left_other.start()

    def other_rest():
        tile[0][1].wait_recv()
        for k in range(2):
            row_other[k].wait_recv()

        @pl.when(has_left)
        def _():
            rightward[1].wait_recv()
            row_left_other.wait_recv()

        pl.when(has_right)(row_right_other.wait_recv)

    for copy in locals_:
        copy.wait()
    put_operator(operators, 0, prop[0], prop[1], 0.5)
    second(0)
    put_operator(operators, 1, prop[0].T, -prop[1].T, 0.5)
    side_zero = jnp.zeros((2, 2, 3 * HALF, HALF), F32)

    @pl.when(jnp.logical_not(has_left))
    def _():
        ext[:, 0] = side_zero

    @pl.when(jnp.logical_not(has_right))
    def _():
        ext[:, 3] = side_zero

    second(1)
    put_operator(operators, 2, table[0], table[1], 2.0)
    put_operator(operators, 3, table[0], -table[1], 1.0)
    zeros[...] = jnp.zeros_like(zeros)
    no_side = (jnp.logical_not(has_left), jnp.logical_not(has_right))
    no_halo = [
        pltpu.make_async_copy(zeros, halo_out.at[:, 0, :, pl.ds(HALF * side, HALF)], local_sem.at[8])
        for side in range(2)
    ]
    for side in range(2):
        pl.when(no_side[side])(no_halo[side].start)
    edge = jnp.zeros((2, 4 * HALF, HALF), F32)
    strip = jnp.zeros((2, HALF, HALF), F32)
    for of in range(2):
        for slot in range(2):
            pad[of, slot, 0] = edge
            pad[of, slot, 4] = edge
            for k in range(1, 4):
                pad[of, slot, k, :, :HALF] = strip
                pad[of, slot, k, :, 3 * HALF :] = strip
    third(0)
    pl.when(first_slice)(own_edges)
    pl.when(second_slice)(other_edges)
    third(1)
    pl.when(first_slice)(own_rest)
    pl.when(second_slice)(other_rest)

    row_at = [jnp.clip(pos[slot, 0] - HALF - HALF * row, 0, HALF) for slot in range(2)]
    col_at = [jnp.clip(pos[slot, 1] - SIDE * col, 0, SIDE - 1) for slot in range(2)]
    block_at = [at // HALF for at in col_at]
    lane_at = [at % HALF for at in col_at]
    lanes = lax.broadcasted_iota(jnp.int32, (SIDE, HALF), 1)

    for k in range(4):
        whole[k] = ext[0, k]

    def footprint(of, slot, part):
        back = lax.rem(HALF - lane_at[slot], HALF)
        turned = [
            pltpu.roll(of[block_at[slot] + j, part, pl.ds(row_at[slot], SIDE), :], back, 1) for j in range(3)
        ]
        near = lanes < HALF - lane_at[slot]
        return [jnp.where(near, turned[j], turned[j + 1]) for j in range(2)]

    real, imag = slice(0, SIDE), slice(SIDE, 2 * SIDE)

    def spread(operator):
        for _ in range(2):
            for slot in range(2):
                wave_real, wave_imag = wave[slot, real], wave[slot, imag]
                for which, value in enumerate((wave_real, wave_imag, 0.5 * wave_real + 0.5 * wave_imag)):
                    high, low = split(value)
                    for at, part in enumerate((high, low, high)):
                        parts[slot, which, :, at * SIDE : (at + 1) * SIDE] = part
                a, b, c = (
                    lax.dot_general(
                        operators[operator, which],
                        parts[slot, which],
                        (((1,), (1,)), ((), ())),
                        preferred_element_type=F32,
                    )
                    for which in range(3)
                )
                wave[slot, real] = a - b
                wave[slot, imag] = (c - a) + (c - b)


    for slot in range(2):
        window_real, window_imag = footprint(whole, slot, 0), footprint(whole, slot, 1)
        for j in range(2):
            at = slice(j * HALF, (j + 1) * HALF)
            probe_real, probe_imag = probe[0, :, at], probe[1, :, at]
            wave[slot, real, at] = window_real[j] * probe_real - window_imag[j] * probe_imag
            wave[slot, imag, at] = window_real[j] * probe_imag + window_imag[j] * probe_real
    spread(0)

    @pl.when(first_slice)
    def _():
        other_edges()
        other_rest()

    @pl.when(second_slice)
    def _():
        own_edges()
        own_rest()

    for slot in range(2):
        window_real, window_imag = footprint(ext.at[1], slot, 0), footprint(ext.at[1], slot, 1)
        for j in range(2):
            at = slice(j * HALF, (j + 1) * HALF)
            wave_real, wave_imag = 4.0 * wave[slot, real, at], 4.0 * wave[slot, imag, at]
            psi[slot, real, at], psi[slot, imag, at] = wave_real, wave_imag
            window[slot, real, at], window[slot, imag, at] = window_real[j], window_imag[j]
            wave[slot, real, at] = window_real[j] * wave_real - window_imag[j] * wave_imag
            wave[slot, imag, at] = window_real[j] * wave_imag + window_imag[j] * wave_real
    spread(0)
    spread(2)
    for slot in range(2):
        far_real, far_imag = wave[slot, real], wave[slot, imag]
        weight = live[slot].astype(F32)
        residual = weight * (far_real * far_real + far_imag * far_imag - intens[slot])
        wave[slot, real] = residual * far_real
        wave[slot, imag] = residual * far_imag
    spread(3)
    spread(1)

    middle = slice(HALF, 3 * HALF)

    def place(of, slot, part, pieces):
        turned = [pltpu.roll(piece, lane_at[slot], 1) for piece in pieces]
        inside = lanes >= lane_at[slot]
        zero = jnp.zeros_like(turned[0])
        pad[of, slot, 1, part, middle] = jnp.where(inside, turned[0], zero)
        pad[of, slot, 2, part, middle] = jnp.where(inside, turned[1], turned[0])
        pad[of, slot, 3, part, middle] = jnp.where(inside, zero, turned[1])

    def collect(of, k, part):
        terms = [
            pad[of, slot, k + 1 - block_at[slot], part, pl.ds(HALF - row_at[slot], 3 * HALF), :] for slot in range(2)
        ]
        return terms[0] + terms[1]

    def gradient(of, slot, lit_real, lit_imag):
        pieces = ([], [])
        for j in range(2):
            at = slice(j * HALF, (j + 1) * HALF)
            back_real, back_imag = 4.0 * wave[slot, real, at], 4.0 * wave[slot, imag, at]
            first, second = lit_real(at), lit_imag(at)
            pieces[0].append(first * back_real + second * back_imag)
            pieces[1].append(first * back_imag - second * back_real)
        place(of, slot, 0, pieces[0])
        place(of, slot, 1, pieces[1])

    away_rows = rows(2 * HALF * (1 - row))
    grad_row = [
        [
            remote(
                GRAD_ROW + 2 * kind + side, grad.at[kind, side, :, away_rows, :], grad_rows.at[kind, side], sibling
            )
            for side in range(2)
        ]
        for kind in range(2)
    ]
    grad_col = [
        [
            remote(
                GRAD_COL + 2 * side + h,
                grad.at[0, side, :, ext_rows[h], :],
                halo_out.at[:, 0, tile_rows[h], pl.ds(HALF * (1 - side), HALF)],
                right if side else left,
            )
            for h in range(2)
        ]
        for side in range(2)
    ]
    has_side = (has_left, has_right)

    def send_halo(of):
        for side in range(2):
            for part in range(2):
                grad[0, side, part] = collect(of, 3 * side, part)
            grad_row[0][side].start()
            pl.when(has_side[side])(grad_col[side][1].start)

    for slot in range(2):
        gradient(1, slot, lambda at: psi[slot, real, at], lambda at: psi[slot, imag, at])
        back_real, back_imag = 4.0 * wave[slot, real], 4.0 * wave[slot, imag]
        window_real, window_imag = window[slot, real], window[slot, imag]
        wave[slot, real] = window_real * back_real + window_imag * back_imag
        wave[slot, imag] = window_real * back_imag - window_imag * back_real
    pl.when(first_slice)(functools.partial(send_halo, 1))
    spread(1)
    for slot in range(2):
        gradient(0, slot, lambda at: probe[0, :, at], lambda at: probe[1, :, at])
    pl.when(second_slice)(functools.partial(send_halo, 0))
    for side in range(2):
        grad_row[0][side].wait_recv()

        @pl.when(has_side[side])
        def _():
            grad[0, side, :, HALF : 2 * HALF] += grad_rows[0, side]
            grad_col[side][0].start()

    for side in range(2):
        for part in range(2):
            grad[1, side, part] = collect(beam, 1 + side, part)
        grad_row[1][side].start()
    for side in range(2):
        at = slice(side * HALF, (side + 1) * HALF)
        core[:, 0, tile_rows[1], at] = grad[1, side, :, ext_rows[1]]
        grad_row[1][side].wait_recv()
        core[:, 0, tile_rows[0], at] = grad[1, side, :, HALF : 2 * HALF] + grad_rows[1, side]
    core_copy = pltpu.make_async_copy(core, core_out, local_sem.at[9])
    core_copy.start()
    for side in range(2):
        pl.when(no_side[side])(no_halo[side].wait)
    core_copy.wait()
    for h in (1, 0):
        for side in range(2):
            pl.when(has_side[side])(grad_col[1 - side][h].wait_recv)

    for h in range(2):
        pl.when(first_slice)(functools.partial(relays_sent, h))
        pl.when(second_slice)(functools.partial(rest_sent, h))
    for k in range(2):
        row_own[k].wait_send()
        row_other[k].wait_send()
        for kind in range(2):
            grad_row[kind][k].wait_send()

    @pl.when(has_left)
    def _():
        row_left_other.wait_send()
        row_left_own.wait_send()
        for h in range(2):
            grad_col[0][h].wait_send()

    @pl.when(has_right)
    def _():
        row_right_other.wait_send()
        row_right_own.wait_send()
        for h in range(2):
            grad_col[1][h].wait_send()


def body(cols, transmission, probe_field, propagator, intensities, positions, live_slots):
    in_hbm = pl.BlockSpec(memory_space=pltpu.HBM)
    plane = (2, SIDE, SIDE)
    stacked = (2, 2 * SIDE, SIDE)
    tile = jax.ShapeDtypeStruct((2, 1, SIDE, SIDE), F32)
    own, halo = pl.pallas_call(
        functools.partial(kernel, cols),
        out_shape=(tile, tile),
        in_specs=[in_hbm] * 7,
        out_specs=(in_hbm, in_hbm),
        scratch_shapes=[
            pltpu.SMEM((2, 2), jnp.int32),
            pltpu.SMEM((2,), jnp.int32),
            pltpu.VMEM((2, 4, 2, 3 * HALF, HALF), F32),
            pltpu.VMEM((4, 2, 3 * HALF, HALF), F32),
            pltpu.VMEM(plane, F32),
            pltpu.VMEM(plane, F32),
            pltpu.VMEM(plane, F32),
            pltpu.VMEM(plane, F32),
            pltpu.VMEM((4, 3, SIDE, 3 * SIDE), BF16),
            pltpu.VMEM((2, 3, SIDE, 3 * SIDE), BF16),
            pltpu.VMEM(stacked, F32),
            pltpu.VMEM(stacked, F32),
            pltpu.VMEM(stacked, F32),
            pltpu.VMEM((2, 2, 5, 2, 4 * HALF, HALF), F32),
            pltpu.VMEM((2, 2, 2, 3 * HALF, HALF), F32),
            pltpu.VMEM((2, 2, 2, HALF, HALF), F32),
            pltpu.VMEM((2, 1, SIDE, SIDE), F32),
            pltpu.VMEM((2, SIDE, HALF), F32),
            pltpu.SemaphoreType.DMA((10,)),
            pltpu.SemaphoreType.DMA((COPIES,)),
            pltpu.SemaphoreType.DMA((COPIES,)),
        ],
        compiler_params=pltpu.CompilerParams(
            collective_id=0, has_side_effects=True, vmem_limit_bytes=60 * 1024 * 1024
        ),
    )(
        positions,
        live_slots,
        transmission,
        probe_field,
        propagator,
        jnp.asarray(transform_table(SIDE)),
        intensities,
    )
    return own + halo


def solution(mesh):
    return jax.shard_map(
        functools.partial(body, mesh.shape["col"]),
        mesh=mesh,
        in_specs=(
            P(None, "beam", "row", "col"),
            P(),
            P(),
            P(("row", "col"), None, None),
            P(("row", "col"), None),
            P(("row", "col")),
        ),
        out_specs=P(None, "beam", "row", "col"),
        check_vma=False,
    )
```

```python
import functools

import jax
import jax.numpy as jnp
import numpy as np
from jax import lax
from jax.experimental import pallas as pl
from jax.experimental.pallas import tpu as pltpu
from jax.sharding import PartitionSpec as P

MESH = pl.DeviceIdType.MESH
SIDE = 256
HALF = 128
F32 = jnp.float32
BF16 = jnp.bfloat16

TILE = 0
LEFTWARD = 4
RIGHTWARD = 6
RELAY_RIGHT = 8
RELAY_BEAM = 10
ROW = 12
GRAD_ROW = 20
GRAD_COL = 24
COPIES = 28


def transform_table(side):
    counter = np.arange(side)
    angles = 2.0 * np.pi / side * (counter[:, None] * counter[None, :] % side)
    return np.stack([np.cos(angles), -np.sin(angles)]).astype(np.float32) / np.float32(np.sqrt(side))


def split(value):
    high = value.astype(BF16)
    return high, (value - high.astype(F32)).astype(BF16)


def put_operator(operators, at, real, imag, scale):
    real, imag = real * scale, imag * scale
    for which, value in enumerate((real, imag, real + imag)):
        high, low = split(value)
        for block, part in enumerate((high, high, low)):
            operators[at, which, :, block * SIDE : (block + 1) * SIDE] = part


def kernel(
    cols,
    pos_hbm,
    live_hbm,
    trans,
    probe_hbm,
    prop_hbm,
    table_hbm,
    intens_hbm,
    core_out,
    halo_out,
    pos,
    live,
    ext,
    whole,
    probe,
    prop,
    table,
    intens,
    operators,
    parts,
    wave,
    psi,
    window,
    pad,
    grad,
    grad_rows,
    core,
    zeros,
    local_sem,
    send_sem,
    recv_sem,
):
    beam, row, col = lax.axis_index("beam"), lax.axis_index("row"), lax.axis_index("col")
    other = 1 - beam
    first_slice, second_slice = beam == 0, beam == 1
    has_left, has_right = col > 0, col < cols - 1
    partner = (other, row, col)
    sibling = (beam, 1 - row, col)
    left = (other, row, jnp.maximum(col - 1, 0))
    right = (other, row, jnp.minimum(col + 1, cols - 1))

    barrier = pltpu.get_barrier_semaphore()

    def greet(peer):
        pl.semaphore_signal(barrier, inc=1, device_id=peer, device_id_type=MESH)

    greet(partner)
    greet(sibling)
    pl.when(has_left)(lambda: greet(left))
    pl.when(has_right)(lambda: greet(right))

    def rows(start):
        return pl.ds(pl.multiple_of(start, HALF), HALF)

    tile_rows = (rows(HALF * (1 - row)), rows(HALF * row))
    ext_rows = (rows(jnp.int32(HALF)), rows(2 * HALF * row))
    sibling_rows = rows(2 * HALF * row)

    locals_ = [
        pltpu.make_async_copy(
            trans.at[:, 0, :, pl.ds(HALF * k, HALF)],
            ext.at[beam, 1 + k, :, pl.ds(pl.multiple_of(HALF * row, HALF), SIDE), :],
            local_sem.at[k],
        )
        for k in range(2)
    ]
    for at, (source, target) in enumerate(
        ((prop_hbm, prop), (table_hbm, table), (probe_hbm, probe), (intens_hbm, intens), (pos_hbm, pos), (live_hbm, live))
    ):
        locals_.append(pltpu.make_async_copy(source, target, local_sem.at[2 + at]))
    for copy in locals_:
        copy.start()

    def remote(at, source, target, peer, arrives=None):
        return pltpu.make_async_remote_copy(
            src_ref=source,
            dst_ref=target,
            send_sem=send_sem.at[at],
            recv_sem=recv_sem.at[at],
            device_id=peer,
            device_id_type=MESH,
        )

    def own(k, h):
        return trans.at[:, 0, tile_rows[h], pl.ds(HALF * k, HALF)]

    def block(of, k, h):
        return ext.at[of, k, :, ext_rows[h], :]

    tile = [[remote(TILE + 2 * k + h, own(k, h), block(beam, 1 + k, h), partner) for h in range(2)] for k in range(2)]
    leftward = [remote(LEFTWARD + h, own(0, h), block(beam, 3, h), left) for h in range(2)]
    rightward = [remote(RIGHTWARD + h, own(1, h), block(beam, 0, h), right) for h in range(2)]
    relay_right = [remote(RELAY_RIGHT + h, block(other, 2, h), block(other, 0, h), right) for h in range(2)]
    relay_beam = [remote(RELAY_BEAM + h, block(other, 3, h), block(other, 3, h), partner) for h in range(2)]

    def to_sibling(at, of, k, source=None):
        return remote(
            ROW + at, block(of, k, 0) if source is None else source, ext.at[of, k, :, sibling_rows, :], sibling
        )

    row_own = [to_sibling(k, beam, 1 + k, own(k, 0)) for k in range(2)]
    row_other = [to_sibling(2 + k, other, 1 + k) for k in range(2)]
    row_left_other = to_sibling(4, other, 0)
    row_left_own = to_sibling(5, beam, 0)
    row_right_other = to_sibling(6, other, 3)
    row_right_own = to_sibling(7, beam, 3)

    pl.semaphore_wait(barrier, 2 + jnp.where(has_left, 1, 0) + jnp.where(has_right, 1, 0))

    def send_rest(h):
        tile[0][h].start()
        pl.when(has_right)(rightward[h].start)

    for h in range(2):
        tile[1][h].start()
        pl.when(has_left)(leftward[h].start)
    for k in range(2):
        row_own[k].start()
    for h in range(2):
        send_rest(h)

    def send_relays(h):
        tile[1][h].wait_recv()
        pl.when(has_right)(relay_right[h].start)
        if h == 0:
            row_other[1].start()

        @pl.when(has_right)
        def _():
            leftward[h].wait_recv()
            relay_beam[h].start()
            if h == 0:
                row_right_other.start()

    def own_edges():
        @pl.when(has_left)
        def _():
            relay_right[0].wait_recv()
            row_left_own.start()

        @pl.when(has_right)
        def _():
            relay_beam[0].wait_recv()
            row_right_own.start()

    def own_rest():
        for k in range(2):
            row_own[k].wait_recv()

        @pl.when(has_left)
        def _():
            relay_right[1].wait_recv()
            row_left_own.wait_recv()

        @pl.when(has_right)
        def _():
            relay_beam[1].wait_recv()
            row_right_own.wait_recv()

    def other_edges():
        tile[0][0].wait_recv()
        row_other[0].start()

        @pl.when(has_left)
        def _():
            rightward[0].wait_recv()
            row_left_other.start()

    def other_rest():
        tile[0][1].wait_recv()
        for k in range(2):
            row_other[k].wait_recv()

        @pl.when(has_left)
        def _():
            rightward[1].wait_recv()
            row_left_other.wait_recv()

        pl.when(has_right)(row_right_other.wait_recv)

    for copy in locals_:
        copy.wait()
    put_operator(operators, 0, prop[0], prop[1], 0.5)
    send_relays(0)
    put_operator(operators, 1, prop[0].T, -prop[1].T, 0.5)
    side_zero = jnp.zeros((2, 2, 3 * HALF, HALF), F32)

    @pl.when(jnp.logical_not(has_left))
    def _():
        ext[:, 0] = side_zero

    @pl.when(jnp.logical_not(has_right))
    def _():
        ext[:, 3] = side_zero

    send_relays(1)
    put_operator(operators, 2, table[0], table[1], 2.0)
    put_operator(operators, 3, table[0], -table[1], 1.0)
    zeros[...] = jnp.zeros_like(zeros)
    no_side = (jnp.logical_not(has_left), jnp.logical_not(has_right))
    no_halo = [
        pltpu.make_async_copy(zeros, halo_out.at[:, 0, :, pl.ds(HALF * side, HALF)], local_sem.at[8])
        for side in range(2)
    ]
    for side in range(2):
        pl.when(no_side[side])(no_halo[side].start)
    edge = jnp.zeros((2, 4 * HALF, HALF), F32)
    strip = jnp.zeros((2, HALF, HALF), F32)
    for of in range(2):
        for slot in range(2):
            pad[of, slot, 0] = edge
            pad[of, slot, 4] = edge
            for k in range(1, 4):
                pad[of, slot, k, :, :HALF] = strip
                pad[of, slot, k, :, 3 * HALF :] = strip
    pl.when(first_slice)(own_edges)
    pl.when(second_slice)(other_edges)
    pl.when(first_slice)(own_rest)
    pl.when(second_slice)(other_rest)

    row_at = [jnp.clip(pos[slot, 0] - HALF - HALF * row, 0, HALF) for slot in range(2)]
    col_at = [jnp.clip(pos[slot, 1] - SIDE * col, 0, SIDE - 1) for slot in range(2)]
    block_at = [at // HALF for at in col_at]
    lane_at = [at % HALF for at in col_at]
    lanes = lax.broadcasted_iota(jnp.int32, (SIDE, HALF), 1)

    for k in range(4):
        whole[k] = ext[0, k]

    def footprint(of, slot, part):
        back = lax.rem(HALF - lane_at[slot], HALF)
        turned = [
            pltpu.roll(of[block_at[slot] + j, part, pl.ds(row_at[slot], SIDE), :], back, 1) for j in range(3)
        ]
        near = lanes < HALF - lane_at[slot]
        return [jnp.where(near, turned[j], turned[j + 1]) for j in range(2)]

    real, imag = slice(0, SIDE), slice(SIDE, 2 * SIDE)

    def spread(operator):
        for _ in range(2):
            for slot in range(2):
                wave_real, wave_imag = wave[slot, real], wave[slot, imag]
                for which, value in enumerate((wave_real, wave_imag, 0.5 * wave_real + 0.5 * wave_imag)):
                    high, low = split(value)
                    for at, part in enumerate((high, low, high)):
                        parts[slot, which, :, at * SIDE : (at + 1) * SIDE] = part
                a, b, c = (
                    lax.dot_general(
                        operators[operator, which],
                        parts[slot, which],
                        (((1,), (1,)), ((), ())),
                        preferred_element_type=F32,
                    )
                    for which in range(3)
                )
                wave[slot, real] = a - b
                wave[slot, imag] = (c - a) + (c - b)


    for slot in range(2):
        window_real, window_imag = footprint(whole, slot, 0), footprint(whole, slot, 1)
        for j in range(2):
            at = slice(j * HALF, (j + 1) * HALF)
            probe_real, probe_imag = probe[0, :, at], probe[1, :, at]
            wave[slot, real, at] = window_real[j] * probe_real - window_imag[j] * probe_imag
            wave[slot, imag, at] = window_real[j] * probe_imag + window_imag[j] * probe_real
    spread(0)

    @pl.when(first_slice)
    def _():
        other_edges()
        other_rest()

    @pl.when(second_slice)
    def _():
        own_edges()
        own_rest()

    for slot in range(2):
        window_real, window_imag = footprint(ext.at[1], slot, 0), footprint(ext.at[1], slot, 1)
        for j in range(2):
            at = slice(j * HALF, (j + 1) * HALF)
            wave_real, wave_imag = 4.0 * wave[slot, real, at], 4.0 * wave[slot, imag, at]
            psi[slot, real, at], psi[slot, imag, at] = wave_real, wave_imag
            window[slot, real, at], window[slot, imag, at] = window_real[j], window_imag[j]
            wave[slot, real, at] = window_real[j] * wave_real - window_imag[j] * wave_imag
            wave[slot, imag, at] = window_real[j] * wave_imag + window_imag[j] * wave_real
    spread(0)
    spread(2)
    for slot in range(2):
        far_real, far_imag = wave[slot, real], wave[slot, imag]
        weight = live[slot].astype(F32)
        residual = weight * (far_real * far_real + far_imag * far_imag - intens[slot])
        wave[slot, real] = residual * far_real
        wave[slot, imag] = residual * far_imag
    spread(3)
    spread(1)

    middle = slice(HALF, 3 * HALF)

    def place(of, slot, part, pieces):
        turned = [pltpu.roll(piece, lane_at[slot], 1) for piece in pieces]
        inside = lanes >= lane_at[slot]
        zero = jnp.zeros_like(turned[0])
        pad[of, slot, 1, part, middle] = jnp.where(inside, turned[0], zero)
        pad[of, slot, 2, part, middle] = jnp.where(inside, turned[1], turned[0])
        pad[of, slot, 3, part, middle] = jnp.where(inside, zero, turned[1])

    def collect(of, k, part):
        terms = [
            pad[of, slot, k + 1 - block_at[slot], part, pl.ds(HALF - row_at[slot], 3 * HALF), :] for slot in range(2)
        ]
        return terms[0] + terms[1]

    def gradient(of, slot, lit_real, lit_imag):
        pieces = ([], [])
        for j in range(2):
            at = slice(j * HALF, (j + 1) * HALF)
            back_real, back_imag = 4.0 * wave[slot, real, at], 4.0 * wave[slot, imag, at]
            first, second = lit_real(at), lit_imag(at)
            pieces[0].append(first * back_real + second * back_imag)
            pieces[1].append(first * back_imag - second * back_real)
        place(of, slot, 0, pieces[0])
        place(of, slot, 1, pieces[1])

    away_rows = rows(2 * HALF * (1 - row))
    grad_row = [
        [
            remote(
                GRAD_ROW + 2 * kind + side, grad.at[kind, side, :, away_rows, :], grad_rows.at[kind, side], sibling
            )
            for side in range(2)
        ]
        for kind in range(2)
    ]
    grad_col = [
        [
            remote(
                GRAD_COL + 2 * side + h,
                grad.at[0, side, :, ext_rows[h], :],
                halo_out.at[:, 0, tile_rows[h], pl.ds(HALF * (1 - side), HALF)],
                right if side else left,
            )
            for h in range(2)
        ]
        for side in range(2)
    ]
    has_side = (has_left, has_right)

    def send_halo(of):
        for side in range(2):
            for part in range(2):
                grad[0, side, part] = collect(of, 3 * side, part)
            grad_row[0][side].start()
            pl.when(has_side[side])(grad_col[side][1].start)

    for slot in range(2):
        gradient(1, slot, lambda at: psi[slot, real, at], lambda at: psi[slot, imag, at])
        back_real, back_imag = 4.0 * wave[slot, real], 4.0 * wave[slot, imag]
        window_real, window_imag = window[slot, real], window[slot, imag]
        wave[slot, real] = window_real * back_real + window_imag * back_imag
        wave[slot, imag] = window_real * back_imag - window_imag * back_real
    pl.when(first_slice)(functools.partial(send_halo, 1))
    spread(1)
    for slot in range(2):
        gradient(0, slot, lambda at: probe[0, :, at], lambda at: probe[1, :, at])
    pl.when(second_slice)(functools.partial(send_halo, 0))
    for side in range(2):
        grad_row[0][side].wait_recv()

        @pl.when(has_side[side])
        def _():
            grad[0, side, :, HALF : 2 * HALF] += grad_rows[0, side]
            grad_col[side][0].start()

    for side in range(2):
        for part in range(2):
            grad[1, side, part] = collect(beam, 1 + side, part)
        grad_row[1][side].start()
    for side in range(2):
        at = slice(side * HALF, (side + 1) * HALF)
        core[:, 0, tile_rows[1], at] = grad[1, side, :, ext_rows[1]]
        grad_row[1][side].wait_recv()
        core[:, 0, tile_rows[0], at] = grad[1, side, :, HALF : 2 * HALF] + grad_rows[1, side]
    core_copy = pltpu.make_async_copy(core, core_out, local_sem.at[9])
    core_copy.start()
    for side in range(2):
        pl.when(no_side[side])(no_halo[side].wait)
    core_copy.wait()
    for h in (1, 0):
        for side in range(2):
            pl.when(has_side[side])(grad_col[1 - side][h].wait_recv)

    for h in range(2):
        tile[1][h].wait_send()
        tile[0][h].wait_send()
        pl.when(has_left)(leftward[h].wait_send)

        @pl.when(has_right)
        def _():
            rightward[h].wait_send()
            relay_right[h].wait_send()
            relay_beam[h].wait_send()

    for k in range(2):
        row_own[k].wait_send()
        row_other[k].wait_send()
        for kind in range(2):
            grad_row[kind][k].wait_send()

    @pl.when(has_left)
    def _():
        row_left_other.wait_send()
        row_left_own.wait_send()
        for h in range(2):
            grad_col[0][h].wait_send()

    @pl.when(has_right)
    def _():
        row_right_other.wait_send()
        row_right_own.wait_send()
        for h in range(2):
            grad_col[1][h].wait_send()


def body(cols, transmission, probe_field, propagator, intensities, positions, live_slots):
    in_hbm = pl.BlockSpec(memory_space=pltpu.HBM)
    plane = (2, SIDE, SIDE)
    stacked = (2, 2 * SIDE, SIDE)
    tile = jax.ShapeDtypeStruct((2, 1, SIDE, SIDE), F32)
    own, halo = pl.pallas_call(
        functools.partial(kernel, cols),
        out_shape=(tile, tile),
        in_specs=[in_hbm] * 7,
        out_specs=(in_hbm, in_hbm),
        scratch_shapes=[
            pltpu.SMEM((2, 2), jnp.int32),
            pltpu.SMEM((2,), jnp.int32),
            pltpu.VMEM((2, 4, 2, 3 * HALF, HALF), F32),
            pltpu.VMEM((4, 2, 3 * HALF, HALF), F32),
            pltpu.VMEM(plane, F32),
            pltpu.VMEM(plane, F32),
            pltpu.VMEM(plane, F32),
            pltpu.VMEM(plane, F32),
            pltpu.VMEM((4, 3, SIDE, 3 * SIDE), BF16),
            pltpu.VMEM((2, 3, SIDE, 3 * SIDE), BF16),
            pltpu.VMEM(stacked, F32),
            pltpu.VMEM(stacked, F32),
            pltpu.VMEM(stacked, F32),
            pltpu.VMEM((2, 2, 5, 2, 4 * HALF, HALF), F32),
            pltpu.VMEM((2, 2, 2, 3 * HALF, HALF), F32),
            pltpu.VMEM((2, 2, 2, HALF, HALF), F32),
            pltpu.VMEM((2, 1, SIDE, SIDE), F32),
            pltpu.VMEM((2, SIDE, HALF), F32),
            pltpu.SemaphoreType.DMA((10,)),
            pltpu.SemaphoreType.DMA((COPIES,)),
            pltpu.SemaphoreType.DMA((COPIES,)),
        ],
        compiler_params=pltpu.CompilerParams(
            collective_id=0, has_side_effects=True, vmem_limit_bytes=60 * 1024 * 1024
        ),
    )(
        positions,
        live_slots,
        transmission,
        probe_field,
        propagator,
        jnp.asarray(transform_table(SIDE)),
        intensities,
    )
    return own + halo


def solution(mesh):
    return jax.shard_map(
        functools.partial(body, mesh.shape["col"]),
        mesh=mesh,
        in_specs=(
            P(None, "beam", "row", "col"),
            P(),
            P(),
            P(("row", "col"), None, None),
            P(("row", "col"), None),
            P(("row", "col")),
        ),
        out_specs=P(None, "beam", "row", "col"),
        check_vma=False,
    )
```

```python
import functools

import jax
import jax.numpy as jnp
import numpy as np
from jax import lax
from jax.experimental import pallas as pl
from jax.experimental.pallas import tpu as pltpu
from jax.sharding import PartitionSpec as P

MESH = pl.DeviceIdType.MESH
SIDE = 256
HALF = 128
F32 = jnp.float32
BF16 = jnp.bfloat16

TILE = 0
LEFTWARD = 4
RIGHTWARD = 6
RELAY_RIGHT = 8
RELAY_BEAM = 10
ROW = 12
SHARE = 20
GRAD_ROW = 21
GRAD_COL = 25
COPIES = 29
LAYER = 8


def transform_table(side):
    counter = np.arange(side)
    angles = 2.0 * np.pi / side * (counter[:, None] * counter[None, :] % side)
    return np.stack([np.cos(angles), -np.sin(angles)]).astype(np.float32) / np.float32(np.sqrt(side))


def split(value):
    high = value.astype(BF16)
    return high, (value - high.astype(F32)).astype(BF16)


def put_operator(operators, at, real, imag, scale):
    real, imag = real * scale, imag * scale
    for which, value in enumerate((real, imag, real + imag)):
        high, low = split(value)
        for block, part in enumerate((high, high, low)):
            operators[at, which, :, block * SIDE : (block + 1) * SIDE] = part


def kernel(
    cols,
    pos_hbm,
    live_hbm,
    trans,
    probe_hbm,
    prop_hbm,
    table_hbm,
    intens_hbm,
    core_out,
    halo_out,
    pos,
    live,
    ext,
    whole,
    probe,
    prop,
    table,
    intens,
    operators,
    parts,
    wave,
    psi,
    window,
    pad,
    grad,
    grad_rows,
    core,
    zeros,
    local_sem,
    send_sem,
    recv_sem,
):
    beam, row, col = lax.axis_index("beam"), lax.axis_index("row"), lax.axis_index("col")
    other = 1 - beam
    first_slice, second_slice = beam == 0, beam == 1
    has_left, has_right = col > 0, col < cols - 1
    shared_here = jnp.logical_and(has_left, lax.rem(col, LAYER) == 0)
    shared_next = jnp.logical_and(has_right, lax.rem(col, LAYER) == LAYER - 1)
    relayed_here = (has_left, jnp.logical_and(has_left, jnp.logical_not(shared_here)))
    relayed_next = (has_right, jnp.logical_and(has_right, jnp.logical_not(shared_next)))
    partner = (other, row, col)
    sibling = (beam, 1 - row, col)
    left = (other, row, jnp.maximum(col - 1, 0))
    right = (other, row, jnp.minimum(col + 1, cols - 1))

    barrier = pltpu.get_barrier_semaphore()

    def greet(peer):
        pl.semaphore_signal(barrier, inc=1, device_id=peer, device_id_type=MESH)

    greet(partner)
    greet(sibling)
    pl.when(has_left)(lambda: greet(left))
    pl.when(has_right)(lambda: greet(right))

    def rows(start):
        return pl.ds(pl.multiple_of(start, HALF), HALF)

    tile_rows = (rows(HALF * (1 - row)), rows(HALF * row))
    ext_rows = (rows(jnp.int32(HALF)), rows(2 * HALF * row))
    sibling_rows = rows(2 * HALF * row)

    locals_ = [
        pltpu.make_async_copy(
            trans.at[:, 0, :, pl.ds(HALF * k, HALF)],
            ext.at[beam, 1 + k, :, pl.ds(pl.multiple_of(HALF * row, HALF), SIDE), :],
            local_sem.at[k],
        )
        for k in range(2)
    ]
    for at, (source, target) in enumerate(
        ((prop_hbm, prop), (table_hbm, table), (probe_hbm, probe), (intens_hbm, intens), (pos_hbm, pos), (live_hbm, live))
    ):
        locals_.append(pltpu.make_async_copy(source, target, local_sem.at[2 + at]))
    for copy in locals_:
        copy.start()

    def remote(at, source, target, peer, arrives=None):
        return pltpu.make_async_remote_copy(
            src_ref=source,
            dst_ref=target,
            send_sem=send_sem.at[at],
            recv_sem=recv_sem.at[at],
            device_id=peer,
            device_id_type=MESH,
        )

    def own(k, h):
        return trans.at[:, 0, tile_rows[h], pl.ds(HALF * k, HALF)]

    def block(of, k, h):
        return ext.at[of, k, :, ext_rows[h], :]

    tile = [[remote(TILE + 2 * k + h, own(k, h), block(beam, 1 + k, h), partner) for h in range(2)] for k in range(2)]
    leftward = [remote(LEFTWARD + h, own(0, h), block(beam, 3, h), left) for h in range(2)]
    rightward = [remote(RIGHTWARD + h, own(1, h), block(beam, 0, h), right) for h in range(2)]
    relay_right = [remote(RELAY_RIGHT + h, block(other, 2, h), block(other, 0, h), right) for h in range(2)]
    quarters = [pl.ds(pl.multiple_of(2 * HALF * row + HALF // 2 * at, HALF // 2), HALF // 2) for at in range(2)]
    relay_part = remote(
        RELAY_RIGHT + 1, ext.at[other, 2, :, quarters[0], :], ext.at[other, 0, :, quarters[0], :], right
    )
    share_block = ext.at[other, 0, :, quarters[1], :]
    share = remote(SHARE, share_block, share_block, partner)
    relay_beam = [remote(RELAY_BEAM + h, block(other, 3, h), block(other, 3, h), partner) for h in range(2)]

    def to_sibling(at, of, k, source=None):
        return remote(
            ROW + at, block(of, k, 0) if source is None else source, ext.at[of, k, :, sibling_rows, :], sibling
        )

    row_own = [to_sibling(k, beam, 1 + k, own(k, 0)) for k in range(2)]
    row_other = [to_sibling(2 + k, other, 1 + k) for k in range(2)]
    row_left_other = to_sibling(4, other, 0)
    row_left_own = to_sibling(5, beam, 0)
    row_right_other = to_sibling(6, other, 3)
    row_right_own = to_sibling(7, beam, 3)

    pl.semaphore_wait(barrier, 2 + jnp.where(has_left, 1, 0) + jnp.where(has_right, 1, 0))

    for h in range(2):
        pl.when(shared_next)(rightward[h].start)
    for h in range(2):
        tile[1][h].start()
        pl.when(has_left)(leftward[h].start)
    for k in range(2):
        row_own[k].start()
    for h in range(2):
        tile[0][h].start()
        pl.when(relayed_next[1])(rightward[h].start)

    def send_relays(h):
        tile[1][h].wait_recv()
        pl.when(relayed_next[h])(relay_right[h].start)
        if h == 1:
            pl.when(shared_next)(relay_part.start)
        if h == 0:
            row_other[1].start()

        @pl.when(has_right)
        def _():
            leftward[h].wait_recv()
            relay_beam[h].start()
            if h == 0:
                row_right_other.start()

    def own_edges():
        @pl.when(has_left)
        def _():
            relay_right[0].wait_recv()
            row_left_own.start()

        @pl.when(has_right)
        def _():
            relay_beam[0].wait_recv()
            row_right_own.start()

    def own_rest():
        for k in range(2):
            row_own[k].wait_recv()

        pl.when(relayed_here[1])(relay_right[1].wait_recv)
        pl.when(shared_here)(relay_part.wait_recv)
        pl.when(shared_here)(share.wait_recv)
        pl.when(has_left)(row_left_own.wait_recv)

        @pl.when(has_right)
        def _():
            relay_beam[1].wait_recv()
            row_right_own.wait_recv()

    def other_edges():
        tile[0][0].wait_recv()
        row_other[0].start()

        @pl.when(has_left)
        def _():
            rightward[0].wait_recv()
            row_left_other.start()

    def other_rest():
        tile[0][1].wait_recv()
        for k in range(2):
            row_other[k].wait_recv()

        pl.when(relayed_here[1])(rightward[1].wait_recv)
        pl.when(has_left)(row_left_other.wait_recv)

        pl.when(has_right)(row_right_other.wait_recv)

    for copy in locals_:
        copy.wait()
    put_operator(operators, 0, prop[0], prop[1], 0.5)
    send_relays(0)
    put_operator(operators, 1, prop[0].T, -prop[1].T, 0.5)
    side_zero = jnp.zeros((2, 2, 3 * HALF, HALF), F32)

    @pl.when(jnp.logical_not(has_left))
    def _():
        ext[:, 0] = side_zero

    @pl.when(jnp.logical_not(has_right))
    def _():
        ext[:, 3] = side_zero

    send_relays(1)

    @pl.when(shared_here)
    def _():
        rightward[1].wait_recv()
        share.start()

    put_operator(operators, 2, table[0], table[1], 2.0)
    put_operator(operators, 3, table[0], -table[1], 1.0)
    zeros[...] = jnp.zeros_like(zeros)
    no_side = (jnp.logical_not(has_left), jnp.logical_not(has_right))
    no_halo = [
        pltpu.make_async_copy(zeros, halo_out.at[:, 0, :, pl.ds(HALF * side, HALF)], local_sem.at[8])
        for side in range(2)
    ]
    for side in range(2):
        pl.when(no_side[side])(no_halo[side].start)
    edge = jnp.zeros((2, 4 * HALF, HALF), F32)
    strip = jnp.zeros((2, HALF, HALF), F32)
    for of in range(2):
        for slot in range(2):
            pad[of, slot, 0] = edge
            pad[of, slot, 4] = edge
            for k in range(1, 4):
                pad[of, slot, k, :, :HALF] = strip
                pad[of, slot, k, :, 3 * HALF :] = strip
    pl.when(first_slice)(own_edges)
    pl.when(second_slice)(other_edges)
    pl.when(first_slice)(own_rest)
    pl.when(second_slice)(other_rest)

    row_at = [jnp.clip(pos[slot, 0] - HALF - HALF * row, 0, HALF) for slot in range(2)]
    col_at = [jnp.clip(pos[slot, 1] - SIDE * col, 0, SIDE - 1) for slot in range(2)]
    block_at = [at // HALF for at in col_at]
    lane_at = [at % HALF for at in col_at]
    lanes = lax.broadcasted_iota(jnp.int32, (SIDE, HALF), 1)

    for k in range(4):
        whole[k] = ext[0, k]

    def footprint(of, slot, part):
        back = lax.rem(HALF - lane_at[slot], HALF)
        turned = [
            pltpu.roll(of[block_at[slot] + j, part, pl.ds(row_at[slot], SIDE), :], back, 1) for j in range(3)
        ]
        near = lanes < HALF - lane_at[slot]
        return [jnp.where(near, turned[j], turned[j + 1]) for j in range(2)]

    real, imag = slice(0, SIDE), slice(SIDE, 2 * SIDE)

    def spread(operator):
        for _ in range(2):
            for slot in range(2):
                wave_real, wave_imag = wave[slot, real], wave[slot, imag]
                for which, value in enumerate((wave_real, wave_imag, 0.5 * wave_real + 0.5 * wave_imag)):
                    high, low = split(value)
                    for at, part in enumerate((high, low, high)):
                        parts[slot, which, :, at * SIDE : (at + 1) * SIDE] = part
                a, b, c = (
                    lax.dot_general(
                        operators[operator, which],
                        parts[slot, which],
                        (((1,), (1,)), ((), ())),
                        preferred_element_type=F32,
                    )
                    for which in range(3)
                )
                wave[slot, real] = a - b
                wave[slot, imag] = (c - a) + (c - b)


    for slot in range(2):
        window_real, window_imag = footprint(whole, slot, 0), footprint(whole, slot, 1)
        for j in range(2):
            at = slice(j * HALF, (j + 1) * HALF)
            probe_real, probe_imag = probe[0, :, at], probe[1, :, at]
            wave[slot, real, at] = window_real[j] * probe_real - window_imag[j] * probe_imag
            wave[slot, imag, at] = window_real[j] * probe_imag + window_imag[j] * probe_real
    spread(0)

    @pl.when(first_slice)
    def _():
        other_edges()
        other_rest()

    @pl.when(second_slice)
    def _():
        own_edges()
        own_rest()

    for slot in range(2):
        window_real, window_imag = footprint(ext.at[1], slot, 0), footprint(ext.at[1], slot, 1)
        for j in range(2):
            at = slice(j * HALF, (j + 1) * HALF)
            wave_real, wave_imag = 4.0 * wave[slot, real, at], 4.0 * wave[slot, imag, at]
            psi[slot, real, at], psi[slot, imag, at] = wave_real, wave_imag
            window[slot, real, at], window[slot, imag, at] = window_real[j], window_imag[j]
            wave[slot, real, at] = window_real[j] * wave_real - window_imag[j] * wave_imag
            wave[slot, imag, at] = window_real[j] * wave_imag + window_imag[j] * wave_real
    spread(0)
    spread(2)
    for slot in range(2):
        far_real, far_imag = wave[slot, real], wave[slot, imag]
        weight = live[slot].astype(F32)
        residual = weight * (far_real * far_real + far_imag * far_imag - intens[slot])
        wave[slot, real] = residual * far_real
        wave[slot, imag] = residual * far_imag
    spread(3)
    spread(1)

    middle = slice(HALF, 3 * HALF)

    def place(of, slot, part, pieces):
        turned = [pltpu.roll(piece, lane_at[slot], 1) for piece in pieces]
        inside = lanes >= lane_at[slot]
        zero = jnp.zeros_like(turned[0])
        pad[of, slot, 1, part, middle] = jnp.where(inside, turned[0], zero)
        pad[of, slot, 2, part, middle] = jnp.where(inside, turned[1], turned[0])
        pad[of, slot, 3, part, middle] = jnp.where(inside, zero, turned[1])

    def collect(of, k, part):
        terms = [
            pad[of, slot, k + 1 - block_at[slot], part, pl.ds(HALF - row_at[slot], 3 * HALF), :] for slot in range(2)
        ]
        return terms[0] + terms[1]

    def gradient(of, slot, lit_real, lit_imag):
        pieces = ([], [])
        for j in range(2):
            at = slice(j * HALF, (j + 1) * HALF)
            back_real, back_imag = 4.0 * wave[slot, real, at], 4.0 * wave[slot, imag, at]
            first, second = lit_real(at), lit_imag(at)
            pieces[0].append(first * back_real + second * back_imag)
            pieces[1].append(first * back_imag - second * back_real)
        place(of, slot, 0, pieces[0])
        place(of, slot, 1, pieces[1])

    away_rows = rows(2 * HALF * (1 - row))
    grad_row = [
        [
            remote(
                GRAD_ROW + 2 * kind + side, grad.at[kind, side, :, away_rows, :], grad_rows.at[kind, side], sibling
            )
            for side in range(2)
        ]
        for kind in range(2)
    ]
    grad_col = [
        [
            remote(
                GRAD_COL + 2 * side + h,
                grad.at[0, side, :, ext_rows[h], :],
                halo_out.at[:, 0, tile_rows[h], pl.ds(HALF * (1 - side), HALF)],
                right if side else left,
            )
            for h in range(2)
        ]
        for side in range(2)
    ]
    has_side = (has_left, has_right)

    def send_halo(of):
        for side in range(2):
            for part in range(2):
                grad[0, side, part] = collect(of, 3 * side, part)
            grad_row[0][side].start()
            pl.when(has_side[side])(grad_col[side][1].start)

    for slot in range(2):
        gradient(1, slot, lambda at: psi[slot, real, at], lambda at: psi[slot, imag, at])
        back_real, back_imag = 4.0 * wave[slot, real], 4.0 * wave[slot, imag]
        window_real, window_imag = window[slot, real], window[slot, imag]
        wave[slot, real] = window_real * back_real + window_imag * back_imag
        wave[slot, imag] = window_real * back_imag - window_imag * back_real
    pl.when(first_slice)(functools.partial(send_halo, 1))
    spread(1)
    for slot in range(2):
        gradient(0, slot, lambda at: probe[0, :, at], lambda at: probe[1, :, at])
    pl.when(second_slice)(functools.partial(send_halo, 0))
    for side in range(2):
        grad_row[0][side].wait_recv()

        @pl.when(has_side[side])
        def _():
            grad[0, side, :, HALF : 2 * HALF] += grad_rows[0, side]
            grad_col[side][0].start()

    for side in range(2):
        for part in range(2):
            grad[1, side, part] = collect(beam, 1 + side, part)
        grad_row[1][side].start()
    for side in range(2):
        at = slice(side * HALF, (side + 1) * HALF)
        core[:, 0, tile_rows[1], at] = grad[1, side, :, ext_rows[1]]
        grad_row[1][side].wait_recv()
        core[:, 0, tile_rows[0], at] = grad[1, side, :, HALF : 2 * HALF] + grad_rows[1, side]
    core_copy = pltpu.make_async_copy(core, core_out, local_sem.at[9])
    core_copy.start()
    for side in range(2):
        pl.when(no_side[side])(no_halo[side].wait)
    core_copy.wait()
    for h in (1, 0):
        for side in range(2):
            pl.when(has_side[side])(grad_col[1 - side][h].wait_recv)

    for h in range(2):
        tile[1][h].wait_send()
        tile[0][h].wait_send()
        pl.when(has_left)(leftward[h].wait_send)

        pl.when(relayed_next[h])(relay_right[h].wait_send)

        @pl.when(has_right)
        def _():
            rightward[h].wait_send()
            relay_beam[h].wait_send()

    pl.when(shared_here)(share.wait_send)
    pl.when(shared_next)(relay_part.wait_send)
    for k in range(2):
        row_own[k].wait_send()
        row_other[k].wait_send()
        for kind in range(2):
            grad_row[kind][k].wait_send()

    @pl.when(has_left)
    def _():
        row_left_other.wait_send()
        row_left_own.wait_send()
        for h in range(2):
            grad_col[0][h].wait_send()

    @pl.when(has_right)
    def _():
        row_right_other.wait_send()
        row_right_own.wait_send()
        for h in range(2):
            grad_col[1][h].wait_send()


def body(cols, transmission, probe_field, propagator, intensities, positions, live_slots):
    in_hbm = pl.BlockSpec(memory_space=pltpu.HBM)
    plane = (2, SIDE, SIDE)
    stacked = (2, 2 * SIDE, SIDE)
    tile = jax.ShapeDtypeStruct((2, 1, SIDE, SIDE), F32)
    own, halo = pl.pallas_call(
        functools.partial(kernel, cols),
        out_shape=(tile, tile),
        in_specs=[in_hbm] * 7,
        out_specs=(in_hbm, in_hbm),
        scratch_shapes=[
            pltpu.SMEM((2, 2), jnp.int32),
            pltpu.SMEM((2,), jnp.int32),
            pltpu.VMEM((2, 4, 2, 3 * HALF, HALF), F32),
            pltpu.VMEM((4, 2, 3 * HALF, HALF), F32),
            pltpu.VMEM(plane, F32),
            pltpu.VMEM(plane, F32),
            pltpu.VMEM(plane, F32),
            pltpu.VMEM(plane, F32),
            pltpu.VMEM((4, 3, SIDE, 3 * SIDE), BF16),
            pltpu.VMEM((2, 3, SIDE, 3 * SIDE), BF16),
            pltpu.VMEM(stacked, F32),
            pltpu.VMEM(stacked, F32),
            pltpu.VMEM(stacked, F32),
            pltpu.VMEM((2, 2, 5, 2, 4 * HALF, HALF), F32),
            pltpu.VMEM((2, 2, 2, 3 * HALF, HALF), F32),
            pltpu.VMEM((2, 2, 2, HALF, HALF), F32),
            pltpu.VMEM((2, 1, SIDE, SIDE), F32),
            pltpu.VMEM((2, SIDE, HALF), F32),
            pltpu.SemaphoreType.DMA((10,)),
            pltpu.SemaphoreType.DMA((COPIES,)),
            pltpu.SemaphoreType.DMA((COPIES,)),
        ],
        compiler_params=pltpu.CompilerParams(
            collective_id=0, has_side_effects=True, vmem_limit_bytes=60 * 1024 * 1024
        ),
    )(
        positions,
        live_slots,
        transmission,
        probe_field,
        propagator,
        jnp.asarray(transform_table(SIDE)),
        intensities,
    )
    return own + halo


def solution(mesh):
    return jax.shard_map(
        functools.partial(body, mesh.shape["col"]),
        mesh=mesh,
        in_specs=(
            P(None, "beam", "row", "col"),
            P(),
            P(),
            P(("row", "col"), None, None),
            P(("row", "col"), None),
            P(("row", "col")),
        ),
        out_specs=P(None, "beam", "row", "col"),
        check_vma=False,
    )
```

```python
import functools

import jax
import jax.numpy as jnp
import numpy as np
from jax import lax
from jax.experimental import pallas as pl
from jax.experimental.pallas import tpu as pltpu
from jax.sharding import PartitionSpec as P

MESH = pl.DeviceIdType.MESH
SIDE = 256
HALF = 128
F32 = jnp.float32
BF16 = jnp.bfloat16

TILE = 0
LEFTWARD = 4
RIGHTWARD = 6
RELAY_RIGHT = 8
RELAY_BEAM = 10
ROW = 12
SHARE = 20
GRAD_ROW = 21
GRAD_COL = 25
COPIES = 29
LAYER = 8


def transform_table(side):
    counter = np.arange(side)
    angles = 2.0 * np.pi / side * (counter[:, None] * counter[None, :] % side)
    return np.stack([np.cos(angles), -np.sin(angles)]).astype(np.float32) / np.float32(np.sqrt(side))


def split(value):
    high = value.astype(BF16)
    return high, (value - high.astype(F32)).astype(BF16)


def put_operator(operators, at, real, imag, scale):
    real, imag = real * scale, imag * scale
    for which, value in enumerate((real, imag, real + imag)):
        high, low = split(value)
        for block, part in enumerate((high, high, low)):
            operators[at, which, :, block * SIDE : (block + 1) * SIDE] = part


def kernel(
    cols,
    pos_hbm,
    live_hbm,
    trans,
    probe_hbm,
    prop_hbm,
    table_hbm,
    intens_hbm,
    core_out,
    halo_out,
    pos,
    live,
    ext,
    whole,
    probe,
    prop,
    table,
    intens,
    operators,
    parts,
    wave,
    psi,
    window,
    pad,
    grad,
    grad_rows,
    core,
    zeros,
    local_sem,
    send_sem,
    recv_sem,
):
    beam, row, col = lax.axis_index("beam"), lax.axis_index("row"), lax.axis_index("col")
    other = 1 - beam
    first_slice, second_slice = beam == 0, beam == 1
    has_left, has_right = col > 0, col < cols - 1
    shared_here = jnp.logical_and(has_left, lax.rem(col, LAYER) == 0)
    shared_next = jnp.logical_and(has_right, lax.rem(col, LAYER) == LAYER - 1)
    relayed_here = (has_left, jnp.logical_and(has_left, jnp.logical_not(shared_here)))
    relayed_next = (has_right, jnp.logical_and(has_right, jnp.logical_not(shared_next)))
    partner = (other, row, col)
    sibling = (beam, 1 - row, col)
    left = (other, row, jnp.maximum(col - 1, 0))
    right = (other, row, jnp.minimum(col + 1, cols - 1))

    barrier = pltpu.get_barrier_semaphore()

    def greet(peer):
        pl.semaphore_signal(barrier, inc=1, device_id=peer, device_id_type=MESH)

    greet(partner)
    greet(sibling)
    pl.when(has_left)(lambda: greet(left))
    pl.when(has_right)(lambda: greet(right))

    def rows(start):
        return pl.ds(pl.multiple_of(start, HALF), HALF)

    tile_rows = (rows(HALF * (1 - row)), rows(HALF * row))
    ext_rows = (rows(jnp.int32(HALF)), rows(2 * HALF * row))
    sibling_rows = rows(2 * HALF * row)

    locals_ = [
        pltpu.make_async_copy(
            trans.at[:, 0, :, pl.ds(HALF * k, HALF)],
            ext.at[beam, 1 + k, :, pl.ds(pl.multiple_of(HALF * row, HALF), SIDE), :],
            local_sem.at[k],
        )
        for k in range(2)
    ]
    for at, (source, target) in enumerate(
        ((prop_hbm, prop), (table_hbm, table), (probe_hbm, probe), (intens_hbm, intens), (pos_hbm, pos), (live_hbm, live))
    ):
        locals_.append(pltpu.make_async_copy(source, target, local_sem.at[2 + at]))
    for copy in locals_:
        copy.start()

    def remote(at, source, target, peer, arrives=None):
        return pltpu.make_async_remote_copy(
            src_ref=source,
            dst_ref=target,
            send_sem=send_sem.at[at],
            recv_sem=recv_sem.at[at],
            device_id=peer,
            device_id_type=MESH,
        )

    def own(k, h):
        return trans.at[:, 0, tile_rows[h], pl.ds(HALF * k, HALF)]

    def block(of, k, h):
        return ext.at[of, k, :, ext_rows[h], :]

    tile = [[remote(TILE + 2 * k + h, own(k, h), block(beam, 1 + k, h), partner) for h in range(2)] for k in range(2)]
    leftward = [remote(LEFTWARD + h, own(0, h), block(beam, 3, h), left) for h in range(2)]
    rightward = [remote(RIGHTWARD + h, own(1, h), block(beam, 0, h), right) for h in range(2)]
    relay_right = [remote(RELAY_RIGHT + h, block(other, 2, h), block(other, 0, h), right) for h in range(2)]
    quarters = [pl.ds(pl.multiple_of(2 * HALF * row + HALF // 2 * at, HALF // 2), HALF // 2) for at in range(2)]
    relay_part = remote(
        RELAY_RIGHT + 1, ext.at[other, 2, :, quarters[0], :], ext.at[other, 0, :, quarters[0], :], right
    )
    share_block = ext.at[other, 0, :, quarters[1], :]
    share = remote(SHARE, share_block, share_block, partner)
    relay_beam = [remote(RELAY_BEAM + h, block(other, 3, h), block(other, 3, h), partner) for h in range(2)]

    def to_sibling(at, of, k, source=None):
        return remote(
            ROW + at, block(of, k, 0) if source is None else source, ext.at[of, k, :, sibling_rows, :], sibling
        )

    row_own = [to_sibling(k, beam, 1 + k, own(k, 0)) for k in range(2)]
    row_other = [to_sibling(2 + k, other, 1 + k) for k in range(2)]
    row_left_other = to_sibling(4, other, 0)
    row_left_own = to_sibling(5, beam, 0)
    row_right_other = to_sibling(6, other, 3)
    row_right_own = to_sibling(7, beam, 3)

    pl.semaphore_wait(barrier, 2 + jnp.where(has_left, 1, 0) + jnp.where(has_right, 1, 0))

    for h in range(2):
        pl.when(shared_next)(rightward[h].start)
    for h in range(2):
        tile[1][h].start()
        pl.when(has_left)(leftward[h].start)
    for k in range(2):
        row_own[k].start()
    for h in range(2):
        tile[0][h].start()
        pl.when(relayed_next[1])(rightward[h].start)

    def send_relays(h):
        tile[1][h].wait_recv()
        pl.when(relayed_next[h])(relay_right[h].start)
        if h == 1:
            pl.when(shared_next)(relay_part.start)
        if h == 0:
            row_other[1].start()

        @pl.when(has_right)
        def _():
            leftward[h].wait_recv()
            relay_beam[h].start()
            if h == 0:
                row_right_other.start()

    def own_edges():
        @pl.when(has_left)
        def _():
            relay_right[0].wait_recv()
            row_left_own.start()

        @pl.when(has_right)
        def _():
            relay_beam[0].wait_recv()
            row_right_own.start()

    def own_rest():
        for k in range(2):
            row_own[k].wait_recv()

        pl.when(relayed_here[1])(relay_right[1].wait_recv)
        pl.when(shared_here)(relay_part.wait_recv)
        pl.when(shared_here)(share.wait_recv)
        pl.when(has_left)(row_left_own.wait_recv)

        @pl.when(has_right)
        def _():
            relay_beam[1].wait_recv()
            row_right_own.wait_recv()

    def other_edges():
        tile[0][0].wait_recv()
        row_other[0].start()

        @pl.when(has_left)
        def _():
            rightward[0].wait_recv()
            row_left_other.start()

    def other_rest():
        tile[0][1].wait_recv()
        for k in range(2):
            row_other[k].wait_recv()

        pl.when(relayed_here[1])(rightward[1].wait_recv)
        pl.when(has_left)(row_left_other.wait_recv)

        pl.when(has_right)(row_right_other.wait_recv)

    for copy in locals_:
        copy.wait()
    put_operator(operators, 0, prop[0], prop[1], 0.5)
    send_relays(0)
    put_operator(operators, 1, prop[0].T, -prop[1].T, 0.5)
    side_zero = jnp.zeros((2, 2, 3 * HALF, HALF), F32)

    @pl.when(jnp.logical_not(has_left))
    def _():
        ext[:, 0] = side_zero

    @pl.when(jnp.logical_not(has_right))
    def _():
        ext[:, 3] = side_zero

    send_relays(1)
    put_operator(operators, 2, table[0], table[1], 2.0)
    put_operator(operators, 3, table[0], -table[1], 1.0)
    zeros[...] = jnp.zeros_like(zeros)
    no_side = (jnp.logical_not(has_left), jnp.logical_not(has_right))
    no_halo = [
        pltpu.make_async_copy(zeros, halo_out.at[:, 0, :, pl.ds(HALF * side, HALF)], local_sem.at[8])
        for side in range(2)
    ]
    for side in range(2):
        pl.when(no_side[side])(no_halo[side].start)
    edge = jnp.zeros((2, 4 * HALF, HALF), F32)
    strip = jnp.zeros((2, HALF, HALF), F32)
    for of in range(2):
        for slot in range(2):
            pad[of, slot, 0] = edge
            pad[of, slot, 4] = edge
            for k in range(1, 4):
                pad[of, slot, k, :, :HALF] = strip
                pad[of, slot, k, :, 3 * HALF :] = strip
    @pl.when(shared_here)
    def _():
        rightward[1].wait_recv()
        share.start()

    pl.when(first_slice)(own_edges)
    pl.when(second_slice)(other_edges)
    pl.when(first_slice)(own_rest)
    pl.when(second_slice)(other_rest)

    row_at = [jnp.clip(pos[slot, 0] - HALF - HALF * row, 0, HALF) for slot in range(2)]
    col_at = [jnp.clip(pos[slot, 1] - SIDE * col, 0, SIDE - 1) for slot in range(2)]
    block_at = [at // HALF for at in col_at]
    lane_at = [at % HALF for at in col_at]
    lanes = lax.broadcasted_iota(jnp.int32, (SIDE, HALF), 1)

    for k in range(4):
        whole[k] = ext[0, k]

    def footprint(of, slot, part):
        back = lax.rem(HALF - lane_at[slot], HALF)
        turned = [
            pltpu.roll(of[block_at[slot] + j, part, pl.ds(row_at[slot], SIDE), :], back, 1) for j in range(3)
        ]
        near = lanes < HALF - lane_at[slot]
        return [jnp.where(near, turned[j], turned[j + 1]) for j in range(2)]

    real, imag = slice(0, SIDE), slice(SIDE, 2 * SIDE)

    def spread(operator):
        for _ in range(2):
            for slot in range(2):
                wave_real, wave_imag = wave[slot, real], wave[slot, imag]
                for which, value in enumerate((wave_real, wave_imag, 0.5 * wave_real + 0.5 * wave_imag)):
                    high, low = split(value)
                    for at, part in enumerate((high, low, high)):
                        parts[slot, which, :, at * SIDE : (at + 1) * SIDE] = part
                a, b, c = (
                    lax.dot_general(
                        operators[operator, which],
                        parts[slot, which],
                        (((1,), (1,)), ((), ())),
                        preferred_element_type=F32,
                    )
                    for which in range(3)
                )
                wave[slot, real] = a - b
                wave[slot, imag] = (c - a) + (c - b)


    for slot in range(2):
        window_real, window_imag = footprint(whole, slot, 0), footprint(whole, slot, 1)
        for j in range(2):
            at = slice(j * HALF, (j + 1) * HALF)
            probe_real, probe_imag = probe[0, :, at], probe[1, :, at]
            wave[slot, real, at] = window_real[j] * probe_real - window_imag[j] * probe_imag
            wave[slot, imag, at] = window_real[j] * probe_imag + window_imag[j] * probe_real
    spread(0)

    @pl.when(first_slice)
    def _():
        other_edges()
        other_rest()

    @pl.when(second_slice)
    def _():
        own_edges()
        own_rest()

    for slot in range(2):
        window_real, window_imag = footprint(ext.at[1], slot, 0), footprint(ext.at[1], slot, 1)
        for j in range(2):
            at = slice(j * HALF, (j + 1) * HALF)
            wave_real, wave_imag = 4.0 * wave[slot, real, at], 4.0 * wave[slot, imag, at]
            psi[slot, real, at], psi[slot, imag, at] = wave_real, wave_imag
            window[slot, real, at], window[slot, imag, at] = window_real[j], window_imag[j]
            wave[slot, real, at] = window_real[j] * wave_real - window_imag[j] * wave_imag
            wave[slot, imag, at] = window_real[j] * wave_imag + window_imag[j] * wave_real
    spread(0)
    spread(2)
    for slot in range(2):
        far_real, far_imag = wave[slot, real], wave[slot, imag]
        weight = live[slot].astype(F32)
        residual = weight * (far_real * far_real + far_imag * far_imag - intens[slot])
        wave[slot, real] = residual * far_real
        wave[slot, imag] = residual * far_imag
    spread(3)
    spread(1)

    middle = slice(HALF, 3 * HALF)

    def place(of, slot, part, pieces):
        turned = [pltpu.roll(piece, lane_at[slot], 1) for piece in pieces]
        inside = lanes >= lane_at[slot]
        zero = jnp.zeros_like(turned[0])
        pad[of, slot, 1, part, middle] = jnp.where(inside, turned[0], zero)
        pad[of, slot, 2, part, middle] = jnp.where(inside, turned[1], turned[0])
        pad[of, slot, 3, part, middle] = jnp.where(inside, zero, turned[1])

    def collect(of, k, part):
        terms = [
            pad[of, slot, k + 1 - block_at[slot], part, pl.ds(HALF - row_at[slot], 3 * HALF), :] for slot in range(2)
        ]
        return terms[0] + terms[1]

    def gradient(of, slot, lit_real, lit_imag):
        pieces = ([], [])
        for j in range(2):
            at = slice(j * HALF, (j + 1) * HALF)
            back_real, back_imag = 4.0 * wave[slot, real, at], 4.0 * wave[slot, imag, at]
            first, second = lit_real(at), lit_imag(at)
            pieces[0].append(first * back_real + second * back_imag)
            pieces[1].append(first * back_imag - second * back_real)
        place(of, slot, 0, pieces[0])
        place(of, slot, 1, pieces[1])

    away_rows = rows(2 * HALF * (1 - row))
    grad_row = [
        [
            remote(
                GRAD_ROW + 2 * kind + side, grad.at[kind, side, :, away_rows, :], grad_rows.at[kind, side], sibling
            )
            for side in range(2)
        ]
        for kind in range(2)
    ]
    grad_col = [
        [
            remote(
                GRAD_COL + 2 * side + h,
                grad.at[0, side, :, ext_rows[h], :],
                halo_out.at[:, 0, tile_rows[h], pl.ds(HALF * (1 - side), HALF)],
                right if side else left,
            )
            for h in range(2)
        ]
        for side in range(2)
    ]
    has_side = (has_left, has_right)

    def send_halo(of):
        for side in range(2):
            for part in range(2):
                grad[0, side, part] = collect(of, 3 * side, part)
            grad_row[0][side].start()
            pl.when(has_side[side])(grad_col[side][1].start)

    for slot in range(2):
        gradient(1, slot, lambda at: psi[slot, real, at], lambda at: psi[slot, imag, at])
        back_real, back_imag = 4.0 * wave[slot, real], 4.0 * wave[slot, imag]
        window_real, window_imag = window[slot, real], window[slot, imag]
        wave[slot, real] = window_real * back_real + window_imag * back_imag
        wave[slot, imag] = window_real * back_imag - window_imag * back_real
    pl.when(first_slice)(functools.partial(send_halo, 1))
    spread(1)
    for slot in range(2):
        gradient(0, slot, lambda at: probe[0, :, at], lambda at: probe[1, :, at])
    pl.when(second_slice)(functools.partial(send_halo, 0))
    for side in range(2):
        grad_row[0][side].wait_recv()

        @pl.when(has_side[side])
        def _():
            grad[0, side, :, HALF : 2 * HALF] += grad_rows[0, side]
            grad_col[side][0].start()

    for side in range(2):
        for part in range(2):
            grad[1, side, part] = collect(beam, 1 + side, part)
        grad_row[1][side].start()
    for side in range(2):
        at = slice(side * HALF, (side + 1) * HALF)
        core[:, 0, tile_rows[1], at] = grad[1, side, :, ext_rows[1]]
        grad_row[1][side].wait_recv()
        core[:, 0, tile_rows[0], at] = grad[1, side, :, HALF : 2 * HALF] + grad_rows[1, side]
    core_copy = pltpu.make_async_copy(core, core_out, local_sem.at[9])
    core_copy.start()
    for side in range(2):
        pl.when(no_side[side])(no_halo[side].wait)
    core_copy.wait()
    for h in (1, 0):
        for side in range(2):
            pl.when(has_side[side])(grad_col[1 - side][h].wait_recv)

    for h in range(2):
        tile[1][h].wait_send()
        tile[0][h].wait_send()
        pl.when(has_left)(leftward[h].wait_send)

        pl.when(relayed_next[h])(relay_right[h].wait_send)

        @pl.when(has_right)
        def _():
            rightward[h].wait_send()
            relay_beam[h].wait_send()

    pl.when(shared_here)(share.wait_send)
    pl.when(shared_next)(relay_part.wait_send)
    for k in range(2):
        row_own[k].wait_send()
        row_other[k].wait_send()
        for kind in range(2):
            grad_row[kind][k].wait_send()

    @pl.when(has_left)
    def _():
        row_left_other.wait_send()
        row_left_own.wait_send()
        for h in range(2):
            grad_col[0][h].wait_send()

    @pl.when(has_right)
    def _():
        row_right_other.wait_send()
        row_right_own.wait_send()
        for h in range(2):
            grad_col[1][h].wait_send()


def body(cols, transmission, probe_field, propagator, intensities, positions, live_slots):
    in_hbm = pl.BlockSpec(memory_space=pltpu.HBM)
    plane = (2, SIDE, SIDE)
    stacked = (2, 2 * SIDE, SIDE)
    tile = jax.ShapeDtypeStruct((2, 1, SIDE, SIDE), F32)
    own, halo = pl.pallas_call(
        functools.partial(kernel, cols),
        out_shape=(tile, tile),
        in_specs=[in_hbm] * 7,
        out_specs=(in_hbm, in_hbm),
        scratch_shapes=[
            pltpu.SMEM((2, 2), jnp.int32),
            pltpu.SMEM((2,), jnp.int32),
            pltpu.VMEM((2, 4, 2, 3 * HALF, HALF), F32),
            pltpu.VMEM((4, 2, 3 * HALF, HALF), F32),
            pltpu.VMEM(plane, F32),
            pltpu.VMEM(plane, F32),
            pltpu.VMEM(plane, F32),
            pltpu.VMEM(plane, F32),
            pltpu.VMEM((4, 3, SIDE, 3 * SIDE), BF16),
            pltpu.VMEM((2, 3, SIDE, 3 * SIDE), BF16),
            pltpu.VMEM(stacked, F32),
            pltpu.VMEM(stacked, F32),
            pltpu.VMEM(stacked, F32),
            pltpu.VMEM((2, 2, 5, 2, 4 * HALF, HALF), F32),
            pltpu.VMEM((2, 2, 2, 3 * HALF, HALF), F32),
            pltpu.VMEM((2, 2, 2, HALF, HALF), F32),
            pltpu.VMEM((2, 1, SIDE, SIDE), F32),
            pltpu.VMEM((2, SIDE, HALF), F32),
            pltpu.SemaphoreType.DMA((10,)),
            pltpu.SemaphoreType.DMA((COPIES,)),
            pltpu.SemaphoreType.DMA((COPIES,)),
        ],
        compiler_params=pltpu.CompilerParams(
            collective_id=0, has_side_effects=True, vmem_limit_bytes=60 * 1024 * 1024
        ),
    )(
        positions,
        live_slots,
        transmission,
        probe_field,
        propagator,
        jnp.asarray(transform_table(SIDE)),
        intensities,
    )
    return own + halo


def solution(mesh):
    return jax.shard_map(
        functools.partial(body, mesh.shape["col"]),
        mesh=mesh,
        in_specs=(
            P(None, "beam", "row", "col"),
            P(),
            P(),
            P(("row", "col"), None, None),
            P(("row", "col"), None),
            P(("row", "col")),
        ),
        out_specs=P(None, "beam", "row", "col"),
        check_vma=False,
    )
```
